256 devices in a mesh: dp: 4 (over z_hi), ctx: 16 (over x, y), head: 4 (over z_lo, core).
Axes of the slice: x: 4, y: 4, z: 8 (z_hi: 4, z_lo: 2; z = z_hi * 2 + z_lo), core: 2. Of those that a mesh axis runs over, the one named last changes fastest.
Arguments:
- queries: bfloat16 [4, 2048, 64, 288], P('dp', 'ctx', 'head'), may hold values from -100 to 100
- latents: bfloat16 [4, 2048, 288], P('dp', 'ctx'), may hold values from -16 to 16
- positions: int32 [4, 2048], P('dp', 'ctx'), may hold values from 0 to 2047, as said below
- lse: float32 [4, 2048, 64], P('dp', 'ctx', 'head'), as said below
- saved_out: bfloat16 [4, 2048, 64, 256], P('dp', 'ctx', 'head'), may hold values from -6 to 6
- out_grad: bfloat16 [4, 2048, 64, 128], P('dp', 'ctx', 'head'), may hold values from -6 to 6
- value_up: bfloat16 [64, 256, 128], P('head'), may hold values from -0.375 to 0.375
Outputs:
- query_grad: bfloat16 [4, 2048, 64, 288], P('dp', 'ctx', 'head')
- latent_grad: float32 [4, 2048, 288], P('dp', 'ctx')
- value_up_grad: float32 [256, 64, 128], P(('dp', 'ctx'), 'head')
The draws below stay inside these ranges and needn't reach their ends.
Inputs may be any that keep to these rules, and one draw needn't show every extreme that they name: For each sequence the 2048 positions are a permutation of 0 to 2047; the 128 slots of each aligned block of 128 slots hold 128 consecutive positions, beginning at a multiple of 128, in some order. lse[b, i, h] is the logarithm of the sum over the slots j visible to i of exp(logits[i, j]).
All inputs are finite; a program needn't handle non-finite values.
Results may differ from the reference program's by a relative error of at most 0.014.
Values may be sent and summed in bfloat16 or wider, within the bound.
No kernel may reach another device: no remote copies, remote signals or barrier semaphores. Data moves between devices by JAX's collectives and lax.ppermute only.
A program may use at most 64 MiB of HBM per device.

```python
import jax
import jax.numpy as jnp
from jax import lax

TOK_DEV = 128
HEADS = 64
LATENT = 256
ROPE = 32
VHEAD = 128
SLAB = 2048
BATCH = 4


def draw_queries(key, part):
    key = jax.random.fold_in(key, 1)
    shape = (BATCH, SLAB, HEADS, LATENT + ROPE)
    values = jnp.clip(jax.random.normal(key, shape, jnp.float32), -6.0, 6.0)
    return values.astype(jnp.bfloat16)


def draw_latents(key, part):
    key = jax.random.fold_in(key, 2)
    shape = (BATCH, SLAB, LATENT + ROPE)
    values = jnp.clip(jax.random.normal(key, shape, jnp.float32), -6.0, 6.0)
    return values.astype(jnp.bfloat16)


def draw_positions(key, part):
    key = jax.random.fold_in(key, 3)
    block_count = SLAB // TOK_DEV
    first_key, second_key = jax.random.split(key)
    order = jax.vmap(lambda inner: jax.random.permutation(inner, block_count))(jax.random.split(first_key, BATCH))
    within = jax.vmap(lambda inner: jax.random.permutation(inner, TOK_DEV))(jax.random.split(second_key, BATCH * block_count))
    within = within.reshape(BATCH, block_count, TOK_DEV)
    return (order[:, :, None] * TOK_DEV + within).reshape(BATCH, SLAB).astype(jnp.int32)


def sequence_lse(query_rows, key_rows, key_pos):
    scaling = (VHEAD + ROPE) ** (-0.5)
    logits = jnp.dot(query_rows, key_rows.T, preferred_element_type=jnp.float32) * scaling
    visible = key_pos[None, :] <= key_pos[:, None]
    row_max = jnp.max(jnp.where(visible, logits, -1e+30), axis=-1)
    row_sum = jnp.sum(jnp.where(visible, jnp.exp(logits - row_max[:, None]), 0.0), axis=-1)
    return row_max + jnp.log(row_sum)


def draw_lse(key, part):
    queries = draw_queries(key, part)
    latents = draw_latents(key, part)
    positions = draw_positions(key, part)
    by_head = jnp.transpose(queries, (2, 0, 1, 3))

    def one_head(query_h):
        return jax.vmap(sequence_lse)(query_h, latents, positions)
    values = lax.map(one_head, by_head)
    return jnp.transpose(values, (1, 2, 0)).astype(jnp.float32)


def with_spikes(array, rng, source, target, shards_of, factor):
    owner, partner = [(jnp.arange(array.shape[axis_at]) // (array.shape[axis_at] // shards_of)).reshape([-1 if axis == axis_at else 1 for axis in range(array.ndim)]) for axis_at in (source, target)]
    chosen = jax.random.permutation(rng, shards_of)[partner]
    strong = (owner == chosen) | (owner == (partner + shards_of // 2) % shards_of)
    return jnp.where(strong, factor * array, array)


def level_of(key, extent, cuts, smallest, high):
    def one(dim, parts):
        draws = jax.random.uniform(jax.random.fold_in(jax.random.fold_in(key, 6), dim), (parts,), jnp.float32, smallest / len(cuts), high / len(cuts))
        return jnp.repeat(jnp.exp(draws), extent[dim] // parts).reshape((-1,) + (1,) * (len(extent) - dim - 1))

    loudness = one(*cuts[0])
    for cut in cuts[1:]:
        loudness = loudness * one(*cut)
    return loudness


def centred(rng, shape, spread, most, shards=(), held_as=jnp.bfloat16):
    entries = spread * jax.random.normal(rng, shape, jnp.float32)
    if shards:
        entries = entries * level_of(rng, shape, shards, -0.22, 0.18)
    return jnp.clip(entries, -most, most).astype(held_as)


def bell_draw_with(key, shape, spread, limit, cuts, heavy, held_as=jnp.bfloat16):
    result = spread * jax.random.normal(key, shape, jnp.float32)
    if cuts:
        result = result * level_of(key, shape, cuts, -0.22, 0.18)
    return jnp.clip(with_spikes(result, jax.random.fold_in(key, 3), *heavy), -limit, limit).astype(held_as)


def setup_inputs(seed: int = 0) -> dict:
    key_list = jax.random.split(jax.random.key(seed), 8)
    queries = draw_queries(jax.random.fold_in(key_list[7], 71), 0)
    latents = draw_latents(jax.random.fold_in(key_list[7], 71), 0)
    positions = draw_positions(jax.random.fold_in(key_list[7], 71), 0)
    lse = draw_lse(jax.random.fold_in(key_list[7], 71), 0)
    saved_out = bell_draw_with(key_list[4], (BATCH, SLAB, HEADS, LATENT), 1.0, 6.0, ((0, 4), (1, 16), (2, 4)), (1, 3, 16, 2.0))
    out_grad = centred(key_list[5], (BATCH, SLAB, HEADS, VHEAD), 1.0, 6.0, ((0, 4), (1, 16), (2, 4)))
    value_up = centred(key_list[6], (HEADS, LATENT, VHEAD), LATENT ** -0.5, 0.375, ((0, 4),))
    return {"queries": queries, "latents": latents, "positions": positions, "lse": lse, "saved_out": saved_out, "out_grad": out_grad, "value_up": value_up}


def head_grads(query_rows, grad_rows, saved_rows, up_matrix, key_rows, key_pos, lse_rows):
    latent_width = up_matrix.shape[0]
    scaling = (VHEAD + ROPE) ** -0.5
    logits = jnp.dot(query_rows, key_rows.T, preferred_element_type=jnp.float32) * scaling
    visible = key_pos[None, :] <= key_pos[:, None]
    lat_grad = jnp.dot(grad_rows, up_matrix.T, preferred_element_type=jnp.float32).astype(jnp.bfloat16)
    row_delta = jnp.sum(lat_grad.astype(jnp.float32) * saved_rows.astype(jnp.float32), axis=-1)
    weights = jnp.where(visible, jnp.exp(logits - lse_rows[:, None]), 0.0)
    dot_value = jnp.dot(lat_grad, key_rows[:, :latent_width].T, preferred_element_type=jnp.float32)
    dlogits = (weights * (dot_value - row_delta[:, None]) * scaling).astype(jnp.bfloat16)
    query_part = jnp.dot(dlogits, key_rows, preferred_element_type=jnp.float32).astype(jnp.bfloat16)
    key_part = jnp.dot(dlogits.T, query_rows, preferred_element_type=jnp.float32)
    value_part = jnp.dot(weights.astype(jnp.bfloat16).T, lat_grad, preferred_element_type=jnp.float32)
    rope_width = key_rows.shape[1] - latent_width
    key_part = key_part + jnp.pad(value_part, ((0, 0), (0, rope_width)))
    return query_part, key_part


def reference(queries, latents, positions, lse, saved_out, out_grad, value_up):
    def one_head(carry, head):
        query_h = lax.dynamic_index_in_dim(queries, head, 2, keepdims=False)
        grad_h = lax.dynamic_index_in_dim(out_grad, head, 2, keepdims=False)
        saved_h = lax.dynamic_index_in_dim(saved_out, head, 2, keepdims=False)
        lse_h = lax.dynamic_index_in_dim(lse, head, 2, keepdims=False)
        up_h = lax.dynamic_index_in_dim(value_up, head, 0, keepdims=False)
        query_part, key_part = jax.vmap(head_grads, in_axes=(0, 0, 0, None, 0, 0, 0))(
            query_h, grad_h, saved_h, up_h, latents, positions, lse_h)
        flat_saved = saved_h.reshape(-1, saved_h.shape[-1])
        flat_grad = grad_h.reshape(-1, grad_h.shape[-1])
        weight_part = jnp.dot(flat_saved.T, flat_grad, preferred_element_type=jnp.float32)
        return carry + key_part, (query_part, weight_part)

    start = jnp.zeros(latents.shape, jnp.float32)
    key_total, (query_parts, weight_parts) = lax.scan(one_head, start, jnp.arange(HEADS, dtype=jnp.int32))
    query_grad = jnp.transpose(query_parts, (1, 2, 0, 3))
    value_up_grad = jnp.transpose(weight_parts, (1, 0, 2))
    return query_grad, key_total, value_up_grad
```

```python
import functools

import jax
import jax.numpy as jnp
from jax import lax
from jax.experimental import pallas as pl
from jax.experimental.pallas import tpu as pltpu
from jax.sharding import PartitionSpec as P

ROPE = 32
VHEAD = 128
LATENT = 256
FULL = LATENT + ROPE
TOK = 128
EXTRA = 16
SCALING = (VHEAD + ROPE) ** -0.5
LOG2E = 1.4426950408889634
FAR = 1e30
F32 = jnp.float32
BF16 = jnp.bfloat16
NT = (((1,), (1,)), ((), ()))
VM = pl.BlockSpec(memory_space=pltpu.VMEM)
PARAMS = pltpu.CompilerParams(vmem_limit_bytes=48 << 20)


def dot(a, b):
    return jnp.dot(a, b, preferred_element_type=F32)


def dot_nt(a, b):
    return lax.dot_general(a, b, NT, preferred_element_type=F32)


def both(ref, pair):
    return jnp.concatenate([ref[2 * pair], ref[2 * pair + 1]], axis=1)


def both_rows(ref, pair):
    return jnp.concatenate([ref[pl.ds(2 * pair, 1), :], ref[pl.ds(2 * pair + 1, 1), :]], axis=1)


def call(kernel, outs, scratch=(), flops=0, nbytes=4 << 20, exps=0):
    return pl.pallas_call(
        kernel,
        out_shape=outs,
        scratch_shapes=list(scratch),
        compiler_params=PARAMS,
        cost_estimate=pl.CostEstimate(flops=flops, bytes_accessed=nbytes, transcendentals=exps),
    )


def shape(dims, dtype):
    return jax.ShapeDtypeStruct(dims, dtype)


def payload_kernel(lat_ref, pos_ref, out_ref):
    pos = pos_ref[...].astype(F32)
    base = jnp.min(pos, axis=1, keepdims=True)
    rank = jnp.broadcast_to(base * (1.0 / TOK), (1, TOK))
    extra = jnp.concatenate([rank, pos - base, jnp.zeros((EXTRA - 2, TOK), F32)], axis=0).astype(BF16)
    for j in range(out_ref.shape[0]):
        out_ref[j, :FULL] = lat_ref[...]
        out_ref[j, FULL:] = extra


def prologue_kernel(
    out_grad, saved, value_up, queries, lat_ref, pos_ref, lse, lat_grad, lat_scaled, delta, weight_part, key_own, dl_own,
    grad_s, saved_s, part_s, key_s,
):
    heads = queries.shape[0]
    groups = part_s.shape[0]
    grad_s[...] = out_grad[...].astype(F32)
    saved_s[0] = saved[:, :VHEAD].astype(F32)
    saved_s[1] = saved[:, VHEAD:].astype(F32)
    width = LATENT // groups

    def one(h, _):
        grad_h = grad_s[pl.ds(h, TOK, stride=heads), :].astype(BF16)
        saved_h = jnp.concatenate([saved_s[c, pl.ds(h, TOK, stride=heads), :].T for c in range(2)], axis=0)
        lat = dot_nt(value_up[h], grad_h)
        scaled = (lat * SCALING).astype(BF16)
        lat_grad[h] = lat.astype(BF16)
        lat_scaled[h] = scaled
        delta[pl.ds(h, 1), :] = jnp.sum(scaled.astype(F32) * saved_h, axis=0, keepdims=True)
        part = dot(saved_h.astype(BF16), grad_h)
        part_s[:, pl.ds(width * h, width), :] = part.reshape(groups, width, VHEAD)
        return 0

    lax.fori_loop(0, heads, one, 0)
    weight_part[...] = part_s[...].astype(BF16)

    key_s[...] = lat_ref[...].T
    pos_q = pos_ref[...].astype(F32)
    pos_k = jnp.broadcast_to(pos_q, (TOK, TOK)).T
    visible = pos_k <= jnp.broadcast_to(pos_q, (TOK, TOK))
    visible = jnp.concatenate([visible, visible], axis=1)
    key_own[...] = jnp.zeros_like(key_own)
    for pair in range(heads // 2):
        q2 = both(queries, pair)
        logits = dot(key_s[...], q2)
        weights = jnp.where(visible, jnp.exp2(logits * (SCALING * LOG2E) - both_rows(lse, pair) * LOG2E), 0.0)
        dot_value = dot(key_s[:, :LATENT], both(lat_scaled, pair))
        dl = (weights * (dot_value - both_rows(delta, pair))).astype(BF16)
        dl_own[:, 256 * pair : 256 * pair + 256] = dl
        key_own[...] += dot_nt(q2, dl)
        key_own[:LATENT] += dot_nt(both(lat_grad, pair), weights.astype(BF16))


def attention_kernel(chunk_blocks, recv, own, queries, lat_grad, lat_scaled, delta, lse, dl_own, own_index, key_acc, dl_all, keys_t, key_s):
    blocks = recv.shape[0]
    heads = queries.shape[0]
    rank_q = own[0, FULL : FULL + 1, :].astype(F32)
    for j in range(blocks):
        keys_t[:, TOK * j : TOK * j + TOK] = recv[j, :FULL]
        key_s[TOK * j : TOK * j + TOK, :] = recv[j, :FULL].T
    key_acc[...] = jnp.zeros_like(key_acc)
    rows = chunk_blocks * TOK
    for chunk in range(blocks // chunk_blocks):
        lo, hi = chunk * rows, chunk * rows + rows
        far = [
            jnp.where(recv[chunk * chunk_blocks + j, FULL : FULL + 1, :].astype(F32) < rank_q, 0.0, FAR)
            for j in range(chunk_blocks)
        ]
        far = [jnp.concatenate([f, f], axis=1) for f in far]

        def one(pair, _):
            q2 = both(queries, pair)
            logits = dot(key_s[lo:hi, :], q2)
            dot_value = dot(key_s[lo:hi, :LATENT], both(lat_scaled, pair))
            lse2 = both_rows(lse, pair) * LOG2E
            delta2 = both_rows(delta, pair)
            weights = jnp.concatenate(
                [
                    jnp.exp2(logits[TOK * j : TOK * j + TOK] * (SCALING * LOG2E) - (lse2 + far[j]))
                    for j in range(chunk_blocks)
                ],
                axis=0,
            )
            dl = (weights * (dot_value - delta2)).astype(BF16)
            dl_all[pair, lo:hi, :] = dl
            lat2 = both(lat_grad, pair)
            key_acc[:LATENT, lo:hi] += dot_nt(
                jnp.concatenate([q2[:LATENT], lat2], axis=1),
                jnp.concatenate([dl, weights.astype(BF16)], axis=1),
            )
            key_acc[LATENT:, lo:hi] += dot_nt(q2[LATENT:], dl)
            return 0

        lax.fori_loop(0, heads // 2, one, 0, unroll=2)
    at = pl.multiple_of(own_index[0] * TOK, TOK)
    for pair in range(heads // 2):
        dl_all[pair, pl.ds(at, TOK), :] = dl_own[:, 256 * pair : 256 * pair + 256]


def pack_kernel(key_acc, key_own, recv, own, weight_recv, out_ref):
    rank_q = own[0, FULL : FULL + 1, :].astype(F32)
    rows = out_ref.shape[1] - FULL
    for j in range(out_ref.shape[0]):
        mine = jnp.where(recv[j, FULL : FULL + 1, :].astype(F32) == rank_q, 1.0, 0.0)
        out_ref[j, :FULL] = (key_acc[:, TOK * j : TOK * j + TOK] + mine * key_own[...]).astype(BF16)
        total = weight_recv[0, rows * j : rows * j + rows].astype(F32)
        for d in range(1, weight_recv.shape[0]):
            total = total + weight_recv[d, rows * j : rows * j + rows].astype(F32)
        out_ref[j, FULL:] = total.astype(BF16)


def query_kernel(keys_t, dl_all, out_ref):
    def one(pair, _):
        grad = dot(keys_t[...], dl_all[pair]).astype(BF16)
        out_ref[2 * pair] = grad[:, :TOK]
        out_ref[2 * pair + 1] = grad[:, TOK:]
        return 0

    lax.fori_loop(0, dl_all.shape[0], one, 0)


def sum_kernel(recv, key_ref, weight_ref, part_s):
    total = recv[0].astype(F32)
    for j in range(1, recv.shape[0]):
        total = total + recv[j].astype(F32)
    key_ref[...] = total[:FULL].astype(BF16)
    part_s[...] = total[FULL:]
    width, heads = weight_ref.shape[0], weight_ref.shape[1]
    for i in range(width):
        weight_ref[i] = part_s[pl.ds(i, heads, stride=width), :]


def body(queries, latents, positions, lse, saved_out, out_grad, value_up):
    n_dp, n_ctx = lax.axis_size("dp"), lax.axis_size("ctx")
    heads = queries.shape[2]
    groups = n_dp * n_ctx
    width = LATENT // groups
    slab = n_ctx * TOK
    pairs = heads // 2
    q_t = jnp.transpose(queries[0], (1, 2, 0))
    lat_t = latents[0].T
    lse_t = lse[0].T
    payload = call(payload_kernel, shape((n_ctx, FULL + EXTRA, TOK), BF16))(lat_t, positions)
    recv = lax.all_to_all(payload, "ctx", 0, 0)

    lat_grad, lat_scaled, delta, weight_part, key_own, dl_own = call(
        prologue_kernel,
        [
            shape((heads, LATENT, TOK), BF16),
            shape((heads, LATENT, TOK), BF16),
            shape((heads, TOK), F32),
            shape((groups, heads * width, VHEAD), BF16),
            shape((FULL, TOK), F32),
            shape((TOK, heads * TOK), BF16),
        ],
        [
            pltpu.VMEM((TOK * heads, VHEAD), F32),
            pltpu.VMEM((2, TOK * heads, VHEAD), F32),
            pltpu.VMEM((groups, heads * width, VHEAD), F32),
            pltpu.VMEM((TOK, FULL), BF16),
        ],
        flops=2 * heads * TOK * TOK * (1400 + 512),
        nbytes=8 << 20,
        exps=heads * TOK * TOK,
    )(
        out_grad[0].reshape(TOK * heads, VHEAD),
        saved_out[0].reshape(TOK * heads, LATENT),
        value_up,
        q_t,
        lat_t,
        positions,
        lse_t,
    )
    weight_recv = lax.all_to_all(weight_part.reshape(n_dp, n_ctx * heads * width, VHEAD), "dp", 0, 0)

    own_index = lax.axis_index("ctx").astype(jnp.int32).reshape(1)
    key_acc, dl_all, keys_t = pl.pallas_call(
        functools.partial(attention_kernel, 4),
        out_shape=[
            shape((FULL, slab), F32),
            shape((pairs, slab, 256), BF16),
            shape((FULL, slab), BF16),
        ],
        in_specs=[VM] * 8 + [pl.BlockSpec(memory_space=pltpu.SMEM)],
        out_specs=[VM] * 3,
        scratch_shapes=[pltpu.VMEM((slab, FULL), BF16)],
        compiler_params=PARAMS,
        cost_estimate=pl.CostEstimate(
            flops=2 * slab * heads * TOK * 1100, bytes_accessed=16 << 20, transcendentals=slab * heads * TOK
        ),
    )(recv, payload[:1], q_t, lat_grad, lat_scaled, delta, lse_t, dl_own, own_index)

    packed = call(pack_kernel, shape((n_ctx, FULL + heads * width, TOK), BF16))(
        key_acc, key_own, recv, payload[:1], weight_recv
    )
    summed = lax.all_to_all(packed, "ctx", 0, 0)
    query_grad = call(
        query_kernel, shape((heads, FULL, TOK), BF16), flops=2 * slab * heads * TOK * FULL, nbytes=12 << 20
    )(keys_t, dl_all)
    key_part, weight_share = call(
        sum_kernel,
        [shape((FULL, TOK), BF16), shape((width, heads, VHEAD), F32)],
        [pltpu.VMEM((heads * width, VHEAD), F32)],
    )(summed)
    key_parts = lax.all_gather(key_part, "head")
    key_grad = jnp.sum(key_parts.astype(F32), axis=0)
    return (jnp.transpose(query_grad, (2, 0, 1))[None], key_grad.T[None], weight_share)


def solution(mesh):
    return jax.shard_map(
        body,
        mesh=mesh,
        in_specs=(
            P("dp", "ctx", "head", None),
            P("dp", "ctx", None),
            P("dp", "ctx"),
            P("dp", "ctx", "head"),
            P("dp", "ctx", "head", None),
            P("dp", "ctx", "head", None),
            P("head", None, None),
        ),
        out_specs=(
            P("dp", "ctx", "head", None),
            P("dp", "ctx", None),
            P(("dp", "ctx"), "head", None),
        ),
        check_vma=False,
    )
```

```python
import functools

import jax
import jax.numpy as jnp
from jax import lax
from jax.experimental import pallas as pl
from jax.experimental.pallas import tpu as pltpu
from jax.sharding import PartitionSpec as P

ROPE = 32
VHEAD = 128
LATENT = 256
FULL = LATENT + ROPE
TOK = 128
HALF = TOK // 2
SCALING = (VHEAD + ROPE) ** -0.5
LOG2E = 1.4426950408889634
FAR = 1e30
ROT = 2 * HALF
RANK = ROT + HALF * ROPE // TOK
BLOCK = RANK + 16
F32 = jnp.float32
BF16 = jnp.bfloat16
FLOPS = (1 << 33, 1 << 33)
NT = (((1,), (1,)), ((), ()))
VM = pl.BlockSpec(memory_space=pltpu.VMEM)
ANY = pl.BlockSpec(memory_space=pl.ANY)
SM = pl.BlockSpec(memory_space=pltpu.SMEM)


def vmem(mib):
    return pltpu.CompilerParams(vmem_limit_bytes=mib << 20)


def cost(flops, nbytes, exps=0):
    return pl.CostEstimate(flops=flops, bytes_accessed=nbytes, transcendentals=exps)


def shape(dims, dtype):
    return jax.ShapeDtypeStruct(dims, dtype)


def near_shape(dims, dtype):
    return pltpu.VMEM(dims, dtype)


def far_shape(dims, dtype):
    return pltpu.HBM(dims, dtype)


def held(x):
    return pltpu.with_memory_space_constraint(x, pltpu.VMEM)


def far_away(x):
    return pltpu.with_memory_space_constraint(x, pltpu.HBM)


def dot(a, b):
    return jnp.dot(a, b, preferred_element_type=F32)


def dot_nt(a, b):
    return lax.dot_general(a, b, NT, preferred_element_type=F32)


def both(ref, pair):
    return jnp.concatenate([ref[2 * pair], ref[2 * pair + 1]], axis=1)


def both_rows(ref, pair):
    return jnp.concatenate([ref[pl.ds(2 * pair, 1), :], ref[pl.ds(2 * pair + 1, 1), :]], axis=1)


def payload_kernel(lat_hbm, pos_hbm, out_hbm, block, lat_s, key_s, pos_s, in_sem, out_sem):
    lat_in = pltpu.make_async_copy(lat_hbm, lat_s, in_sem.at[0])
    pos_in = pltpu.make_async_copy(pos_hbm, pos_s, in_sem.at[1])
    lat_in.start()
    pos_in.start()
    pos_in.wait()
    base = jnp.min(pos_s[...].astype(F32), axis=1, keepdims=True)
    block[RANK:] = jnp.broadcast_to(base * (1.0 / TOK), (BLOCK - RANK, TOK)).astype(BF16)
    lat_in.wait()
    key_s[...] = lat_s[...].T
    half = key_s[pl.ds(pl.multiple_of(lax.rem(lax.axis_index("head"), 2) * HALF, HALF), HALF), :]
    block[:HALF] = half[:, :TOK]
    block[HALF:ROT] = half[:, TOK:LATENT]
    rot = half[:, LATENT:].astype(F32)
    block[ROT:RANK] = jnp.concatenate([rot[16 * g : 16 * g + 16] for g in range(HALF // 16)], axis=1).astype(BF16)
    copies = [pltpu.make_async_copy(block, out_hbm.at[j], out_sem.at[j]) for j in range(out_hbm.shape[0])]
    for copy in copies:
        copy.start()
    for copy in copies:
        copy.wait()


def prologue_kernel(out_grad_hbm, saved_hbm, up_hbm, q_hbm, lat_hbm, pos_hbm, lse_hbm, *rest):
    start, lat_hbm_out, scaled_hbm, delta_hbm, own_hbm, query_hbm, parts_hbm = rest[:7]
    queries, lse, lat_grad, lat_scaled, delta = rest[7:12]
    out_grad, saved, value_up, lat_ref, pos_ref, grad_s, saved_s, part_s, parts, key_s = rest[-15:-5]
    key_own, own_s, query_own, sem, out_sem = rest[-5:]
    core = lax.rem(lax.axis_index("head"), 2)
    moves = [
        (out_grad_hbm, out_grad),
        (saved_hbm, saved),
        (up_hbm, value_up),
        (q_hbm, queries),
        (lat_hbm, lat_ref),
        (pos_hbm, pos_ref),
        (lse_hbm, lse),
    ]
    copies = [pltpu.make_async_copy(src, dst, sem.at[i]) for i, (src, dst) in enumerate(moves)]
    for copy in copies:
        copy.start()
    heads = queries.shape[0]
    n_ctx, n_dp = part_s.shape[:2]
    width = LATENT // (n_ctx * n_dp)
    copies[0].wait()
    grad_s[...] = out_grad[...].astype(F32)
    copies[1].wait()
    saved_s[0] = saved[:, :VHEAD].astype(F32)
    saved_s[1] = saved[:, VHEAD:].astype(F32)
    for copy in copies[2:]:
        copy.wait()

    def one(h, _):
        grad_h = grad_s[pl.ds(h, TOK, stride=heads), :].astype(BF16)
        saved_h = jnp.concatenate([saved_s[c, pl.ds(h, TOK, stride=heads), :].T for c in range(2)], axis=0)
        lat = dot_nt(value_up[h], grad_h)
        scaled = (lat * SCALING).astype(BF16)
        lat_grad[h] = lat.astype(BF16)
        lat_scaled[h] = scaled
        delta[pl.ds(h, 1), :] = jnp.sum(scaled.astype(F32) * saved_h, axis=0, keepdims=True)
        part = dot(saved_h.astype(BF16), grad_h)
        for d in range(n_dp):
            rows = part[d * n_ctx * width : (d + 1) * n_ctx * width]
            part_s[:, d, pl.ds(width * h, width), :] = rows.reshape(n_ctx, width, VHEAD)
        return 0

    lax.fori_loop(0, heads, one, 0, unroll=4)
    start[...] = jnp.zeros_like(start)
    outs = [
        (parts, parts_hbm),
        (lat_grad, lat_hbm_out),
        (lat_scaled, scaled_hbm),
        (delta, delta_hbm),
        (own_s, own_hbm),
        (query_own, query_hbm),
    ]
    outs = [pltpu.make_async_copy(src, dst, out_sem.at[i]) for i, (src, dst) in enumerate(outs)]
    parts[...] = part_s[...].astype(BF16)
    for copy in outs[:4]:
        copy.start()

    key_s[...] = lat_ref[...].T
    pos_q = pos_ref[...].astype(F32)
    pos_k = jnp.broadcast_to(pos_q, (TOK, TOK)).T
    visible = pos_k <= jnp.broadcast_to(pos_q, (TOK, TOK))
    visible = jnp.concatenate([visible, visible], axis=1)
    key_own[...] = jnp.zeros_like(key_own)
    for pair in range(heads // 2):
        q2 = both(queries, pair)
        logits = dot(key_s[...], q2)
        weights = jnp.where(visible, jnp.exp2(logits * (SCALING * LOG2E) - both_rows(lse, pair) * LOG2E), 0.0)
        dot_value = dot(key_s[:, :LATENT], both(lat_scaled, pair))
        dl = (weights * (dot_value - both_rows(delta, pair))).astype(BF16)
        query_own[pair] = dot(lat_ref[...], dl)
        key_own[...] += dot_nt(q2, dl)
        key_own[:LATENT] += dot_nt(both(lat_grad, pair), weights.astype(BF16))
    own = key_own[...]
    own_s[...] = jnp.where(core == 0, own, jnp.concatenate([own[:, HALF:], own[:, :HALF]], axis=1))
    for copy in outs[4:]:
        copy.start()
    for copy in outs:
        copy.wait()


def attention_kernel(
    recv_hbm, q_hbm, lse_hbm, lat_hbm, scaled_hbm, delta_hbm, after, query_hbm, key_acc, done,
    recv, queries, lse, lat_grad, lat_scaled, delta, key_s, keys_t, query_s, sem, in_sem,
):
    heads = queries.shape[0]
    count = key_s.shape[0] // HALF
    quarter = count // 4
    moves = [(recv_hbm.at[i * quarter : (i + 1) * quarter], recv.at[i * quarter : (i + 1) * quarter]) for i in range(4)]
    moves += [(lse_hbm, lse), (delta_hbm, delta)]
    near = heads // 2
    for lo in (0, near):
        pieces = ((q_hbm, queries), (scaled_hbm, lat_scaled), (lat_hbm, lat_grad))
        moves += [(src.at[lo : lo + near], dst.at[lo : lo + near]) for src, dst in pieces]
    copies = [pltpu.make_async_copy(src, dst, in_sem.at[i]) for i, (src, dst) in enumerate(moves)]
    for copy in copies:
        copy.start()
    own = lax.axis_index("ctx")
    key_acc[...] = jnp.zeros_like(key_acc)
    for j in range(count):
        if j % quarter == 0:
            copies[j // quarter].wait()
        lo = HALF * j
        key_s[lo : lo + HALF, :TOK] = recv[j, :HALF]
        key_s[lo : lo + HALF, TOK:LATENT] = recv[j, HALF:ROT]
        rot = recv[j, ROT:RANK].astype(F32)
        for g in range(HALF // 16):
            key_s[lo + 16 * g : lo + 16 * g + 16, LATENT:] = rot[:, ROPE * g : ROPE * g + ROPE].astype(BF16)
        if j % 2:
            keys_t[:, lo - HALF : lo + HALF] = key_s[lo - HALF : lo + HALF, :].T
    rank_q = recv[own, RANK : RANK + 1, :].astype(F32)
    far = []
    for j in range(count):
        one_far = jnp.where(recv[j, RANK : RANK + 1, :].astype(F32) < rank_q, 0.0, FAR)
        far.append(jnp.concatenate([one_far, one_far], axis=1))
    def one(pair, _):
        q2 = both(queries, pair)
        logits = dot(key_s[...], q2)
        dot_value = dot(key_s[:, :LATENT], both(lat_scaled, pair))
        lse2 = both_rows(lse, pair) * LOG2E
        delta2 = both_rows(delta, pair)
        weights = jnp.concatenate(
            [
                jnp.exp2(logits[HALF * j : HALF * j + HALF] * (SCALING * LOG2E) - (lse2 + far[j]))
                for j in range(count)
            ],
            axis=0,
        )
        dl = (weights * (dot_value - delta2)).astype(BF16)
        query_s[pair] = dot(keys_t[...], dl)
        pltpu.make_async_copy(query_s.at[pair], query_hbm.at[pair], sem.at[pair]).start()
        key_acc[:LATENT] += dot_nt(
            jnp.concatenate([q2[:LATENT], both(lat_grad, pair)], axis=1),
            jnp.concatenate([dl, weights.astype(BF16)], axis=1),
        )
        key_acc[LATENT:] += dot_nt(q2[LATENT:], dl)
        return 0

    for i in range(2):
        for copy in copies[4 + 5 * i : 9 + 3 * i]:
            copy.wait()
        lax.fori_loop(near // 2 * i, near // 2 * (i + 1), one, 0, unroll=near // 2)
    done[...] = after[: done.shape[0]]
    for pair in range(heads // 2):
        pltpu.make_async_copy(query_s.at[pair], query_hbm.at[pair], sem.at[pair]).wait()


def pack_kernel(mine, other, own_ref, after, out_ref):
    del after
    own = lax.axis_index("ctx")
    for j in range(out_ref.shape[0]):
        lo = HALF * j
        total = jnp.concatenate([mine[:, lo : lo + HALF], other[:, lo : lo + HALF]], axis=1)
        total = total + jnp.where(own == j, 1.0, 0.0) * own_ref[...]
        out_ref[j] = total.astype(BF16)


def weight_kernel(recv, friend_ref, keep_ref):
    total = recv[0].astype(F32)
    for j in range(1, recv.shape[0]):
        total = total + recv[j].astype(F32)
    dp = lax.axis_index("dp")
    friend = dp + 1 - 2 * lax.rem(dp, 2)
    for ref, index in ((friend_ref, friend), (keep_ref, dp)):
        for i, part in enumerate((index, recv.shape[1] - 1 - index)):
            chosen = total[0]
            for d in range(1, recv.shape[1]):
                chosen = jnp.where(part == d, total[d], chosen)
            ref[i] = chosen.astype(BF16)


def middle_kernel(keep, recv, stay_ref, send_ref):
    total = keep[...].astype(F32) + recv[...].astype(F32)
    stay_ref[...] = total[0]
    send_ref[...] = total[1].astype(BF16)


def query_kernel(own, mine, other, out_ref):
    for i in range(own.shape[0]):
        grad = own[i] + mine[i] + other[i]
        out_ref[2 * i] = grad[:, :TOK].astype(BF16)
        out_ref[2 * i + 1] = grad[:, TOK:].astype(BF16)


def sum_kernel(recv, stay, weight_recv, key_ref, weight_ref, part_s):
    total = recv[0].astype(F32)
    for j in range(1, recv.shape[0]):
        total = total + recv[j].astype(F32)
    key_ref[...] = total.astype(BF16)
    part_s[...] = stay[...] + weight_recv[...].astype(F32)
    width, heads = weight_ref.shape[0], weight_ref.shape[1]
    for i in range(width):
        weight_ref[i] = part_s[pl.ds(i, heads, stride=width), :]


def last_kernel(parts, out_ref):
    sides = []
    for core in range(2):
        total = parts[core].astype(F32)
        for other in range(core + 2, parts.shape[0], 2):
            total = total + parts[other].astype(F32)
        sides.append(total)
    out_ref[...] = sides[0] + jnp.concatenate([sides[1][:, HALF:], sides[1][:, :HALF]], axis=1)


def body(queries, latents, positions, lse, saved_out, out_grad, value_up):
    n_dp, n_ctx, n_head = lax.axis_size("dp"), lax.axis_size("ctx"), lax.axis_size("head")
    heads = queries.shape[2]
    groups = n_dp * n_ctx
    width = LATENT // groups
    pairs = heads // 2
    q_t = far_away(jnp.transpose(queries[0], (1, 2, 0)))
    lat_t = far_away(latents[0].T)
    lse_t = far_away(lse[0].T)
    positions = far_away(positions)
    def core_swap(x):
        return lax.ppermute(x, "head", [(i, i ^ 1) for i in range(n_head)])

    payload = pl.pallas_call(
        payload_kernel,
        out_shape=shape((n_ctx, BLOCK, TOK), BF16),
        in_specs=[ANY, ANY],
        out_specs=ANY,
        scratch_shapes=[
            pltpu.VMEM((BLOCK, TOK), BF16),
            pltpu.VMEM((FULL, TOK), BF16),
            pltpu.VMEM((TOK, FULL), BF16),
            pltpu.VMEM((1, TOK), jnp.int32),
            pltpu.SemaphoreType.DMA((2,)),
            pltpu.SemaphoreType.DMA((n_ctx,)),
        ],
        compiler_params=vmem(2),
    )(lat_t, positions)
    recv_mine = lax.all_to_all(payload, "ctx", 0, 0)

    part_rows = heads * width
    start, lat_grad, lat_scaled, delta, key_own, query_own, parts = pl.pallas_call(
        prologue_kernel,
        out_shape=[
            near_shape((8, TOK), F32),
            far_shape((heads, LATENT, TOK), BF16),
            far_shape((heads, LATENT, TOK), BF16),
            far_shape((heads, TOK), F32),
            far_shape((FULL, TOK), F32),
            far_shape((pairs, FULL, 2 * TOK), F32),
            far_shape((n_ctx, n_dp, part_rows, VHEAD), BF16),
        ],
        in_specs=[ANY] * 7,
        out_specs=[VM] + [ANY] * 6,
        scratch_shapes=[
            pltpu.VMEM((heads, FULL, TOK), BF16),
            pltpu.VMEM((heads, TOK), F32),
            pltpu.VMEM((heads, LATENT, TOK), BF16),
            pltpu.VMEM((heads, LATENT, TOK), BF16),
            pltpu.VMEM((heads, TOK), F32),
            pltpu.VMEM((TOK * heads, VHEAD), BF16),
            pltpu.VMEM((TOK * heads, LATENT), BF16),
            pltpu.VMEM((heads, LATENT, VHEAD), BF16),
            pltpu.VMEM((FULL, TOK), BF16),
            pltpu.VMEM((1, TOK), jnp.int32),
            pltpu.VMEM((TOK * heads, VHEAD), F32),
            pltpu.VMEM((2, TOK * heads, VHEAD), F32),
            pltpu.VMEM((n_ctx, n_dp, part_rows, VHEAD), F32),
            pltpu.VMEM((n_ctx, n_dp, part_rows, VHEAD), BF16),
            pltpu.VMEM((TOK, FULL), BF16),
            pltpu.VMEM((FULL, TOK), F32),
            pltpu.VMEM((FULL, TOK), F32),
            pltpu.VMEM((pairs, FULL, 2 * TOK), F32),
            pltpu.SemaphoreType.DMA((7,)),
            pltpu.SemaphoreType.DMA((6,)),
        ],
        compiler_params=vmem(28),
        cost_estimate=cost(2 * heads * TOK * TOK * 1900, 8 << 20, heads * TOK * TOK),
    )(
        far_away(out_grad[0].reshape(TOK * heads, VHEAD)),
        far_away(saved_out[0].reshape(TOK * heads, LATENT)),
        far_away(value_up),
        q_t,
        lat_t,
        positions,
        lse_t,
    )
    recv_other = core_swap(recv_mine)

    def attend(recv, after, flops):
        rows = n_ctx * HALF
        return pl.pallas_call(
            attention_kernel,
            out_shape=[
                far_shape((pairs, FULL, 2 * TOK), F32),
                near_shape((FULL, rows), F32),
                near_shape((8, TOK), F32),
            ],
            in_specs=[ANY] * 6 + [VM],
            out_specs=[ANY, VM, VM],
            scratch_shapes=[
                pltpu.VMEM((n_ctx, BLOCK, TOK), BF16),
                pltpu.VMEM((heads, FULL, TOK), BF16),
                pltpu.VMEM((heads, TOK), F32),
                pltpu.VMEM((heads, LATENT, TOK), BF16),
                pltpu.VMEM((heads, LATENT, TOK), BF16),
                pltpu.VMEM((heads, TOK), F32),
                pltpu.VMEM((rows, FULL), BF16),
                pltpu.VMEM((FULL, rows), BF16),
                pltpu.VMEM((pairs, FULL, 2 * TOK), F32),
                pltpu.SemaphoreType.DMA((pairs,)),
                pltpu.SemaphoreType.DMA((12,)),
            ],
            compiler_params=vmem(24),
            cost_estimate=cost(flops, 1 << 16),
        )(recv, q_t, lse_t, far_away(lat_grad), far_away(lat_scaled), far_away(delta), held(after))

    query_1, sum_1, step = attend(recv_mine, start, FLOPS[0])
    query_2, sum_2, step = attend(recv_other, step, FLOPS[1])

    weight_ctx = lax.all_to_all(parts, "ctx", 0, 0)
    send_1, keep_1 = pl.pallas_call(
        weight_kernel,
        out_shape=[
            shape((2, part_rows, VHEAD), BF16),
            shape((2, part_rows, VHEAD), BF16),
        ],
        in_specs=[VM],
        out_specs=[VM] * 2,
        compiler_params=vmem(4),
        cost_estimate=cost(1 << 16, 1 << 16),
    )(weight_ctx)

    packed = pl.pallas_call(
        pack_kernel,
        out_shape=shape((n_ctx, FULL, TOK), BF16),
        in_specs=[VM] * 3 + [ANY],
        out_specs=VM,
        compiler_params=vmem(6),
    )(held(sum_1), held(sum_2), key_own, weight_ctx)
    summed = lax.all_to_all(packed, "ctx", 0, 0)

    recv_1 = lax.ppermute(send_1, "dp", [(i, i ^ 1) for i in range(n_dp)])
    stay, send_2 = pl.pallas_call(
        middle_kernel,
        out_shape=[shape((part_rows, VHEAD), F32), shape((part_rows, VHEAD), BF16)],
        in_specs=[VM] * 2,
        out_specs=[VM] * 2,
        compiler_params=vmem(2),
        cost_estimate=cost(1 << 16, 1 << 16),
    )(keep_1, recv_1)
    recv_2 = lax.ppermute(send_2, "dp", [(i, n_dp - 1 - i) for i in range(n_dp)])
    query_grad = pl.pallas_call(
        query_kernel,
        out_shape=shape((heads, FULL, TOK), BF16),
        grid=(4,),
        in_specs=[pl.BlockSpec((pairs // 4, FULL, 2 * TOK), lambda p: (p, 0, 0))] * 3,
        out_specs=pl.BlockSpec((heads // 4, FULL, TOK), lambda p: (p, 0, 0)),
        compiler_params=vmem(12),
        cost_estimate=cost(1 << 33, 12 << 20),
    )(*[far_away(x) for x in (query_own, query_1, query_2)])
    key_part, weight_share = pl.pallas_call(
        sum_kernel,
        out_shape=[shape((FULL, TOK), BF16), shape((width, heads, VHEAD), F32)],
        in_specs=[VM] * 3,
        out_specs=[VM] * 2,
        scratch_shapes=[pltpu.VMEM((heads * width, VHEAD), F32)],
        compiler_params=vmem(4),
    )(summed, stay, recv_2)
    key_grad = pl.pallas_call(
        last_kernel,
        out_shape=shape((FULL, TOK), F32),
        in_specs=[VM],
        out_specs=VM,
        compiler_params=vmem(2),
    )(lax.all_gather(key_part, "head"))
    return (jnp.transpose(query_grad, (2, 0, 1))[None], key_grad.T[None], weight_share)


def solution(mesh):
    return jax.shard_map(
        body,
        mesh=mesh,
        in_specs=(
            P("dp", "ctx", "head", None),
            P("dp", "ctx", None),
            P("dp", "ctx"),
            P("dp", "ctx", "head"),
            P("dp", "ctx", "head", None),
            P("dp", "ctx", "head", None),
            P("head", None, None),
        ),
        out_specs=(
            P("dp", "ctx", "head", None),
            P("dp", "ctx", None),
            P(("dp", "ctx"), "head", None),
        ),
        check_vma=False,
    )
```

```python
import functools

import jax
import jax.numpy as jnp
from jax import lax
from jax.experimental import pallas as pl
from jax.experimental.pallas import tpu as pltpu
from jax.sharding import PartitionSpec as P

ROPE = 32
VHEAD = 128
LATENT = 256
FULL = LATENT + ROPE
TOK = 128
HALF = TOK // 2
SCALING = (VHEAD + ROPE) ** -0.5
LOG2E = 1.4426950408889634
FAR = 1e30
ROT = 2 * HALF
RANK = ROT + HALF * ROPE // TOK
BLOCK = RANK + 16
SPLIT = FULL // 2
F32 = jnp.float32
BF16 = jnp.bfloat16
NT = (((1,), (1,)), ((), ()))
VM = pl.BlockSpec(memory_space=pltpu.VMEM)
ANY = pl.BlockSpec(memory_space=pl.ANY)
SM = pl.BlockSpec(memory_space=pltpu.SMEM)


def vmem(mib):
    return pltpu.CompilerParams(vmem_limit_bytes=mib << 20)


def cost(flops, nbytes, exps=0):
    return pl.CostEstimate(flops=flops, bytes_accessed=nbytes, transcendentals=exps)


def shape(dims, dtype):
    return jax.ShapeDtypeStruct(dims, dtype)


def near_shape(dims, dtype):
    return pltpu.VMEM(dims, dtype)


def far_shape(dims, dtype):
    return pltpu.HBM(dims, dtype)


def held(x):
    return pltpu.with_memory_space_constraint(x, pltpu.VMEM)


def far_away(x):
    return pltpu.with_memory_space_constraint(x, pltpu.HBM)


def dot(a, b):
    return jnp.dot(a, b, preferred_element_type=F32)


def dot_nt(a, b):
    return lax.dot_general(a, b, NT, preferred_element_type=F32)


def both(ref, pair):
    return jnp.concatenate([ref[2 * pair], ref[2 * pair + 1]], axis=1)


def both_rows(ref, pair):
    return jnp.concatenate([ref[pl.ds(2 * pair, 1), :], ref[pl.ds(2 * pair + 1, 1), :]], axis=1)


def payload_kernel(lat_hbm, pos_hbm, out_hbm, block, lat_s, key_s, pos_s, in_sem, out_sem):
    lat_in = pltpu.make_async_copy(lat_hbm, lat_s, in_sem.at[0])
    pos_in = pltpu.make_async_copy(pos_hbm, pos_s, in_sem.at[1])
    lat_in.start()
    pos_in.start()
    pos_in.wait()
    base = jnp.min(pos_s[...].astype(F32), axis=1, keepdims=True)
    block[RANK:] = jnp.broadcast_to(base * (1.0 / TOK), (BLOCK - RANK, TOK)).astype(BF16)
    lat_in.wait()
    key_s[...] = lat_s[...].T
    half = key_s[pl.ds(pl.multiple_of(lax.rem(lax.axis_index("head"), 2) * HALF, HALF), HALF), :]
    block[:HALF] = half[:, :TOK]
    block[HALF:ROT] = half[:, TOK:LATENT]
    rot = half[:, LATENT:].astype(F32)
    block[ROT:RANK] = jnp.concatenate([rot[16 * g : 16 * g + 16] for g in range(HALF // 16)], axis=1).astype(BF16)
    copies = [pltpu.make_async_copy(block, out_hbm.at[j], out_sem.at[j]) for j in range(out_hbm.shape[0])]
    for copy in copies:
        copy.start()
    for copy in copies:
        copy.wait()


def prologue_kernel(out_grad_hbm, saved_hbm, up_hbm, q_hbm, lat_hbm, pos_hbm, lse_hbm, *rest):
    start, lat_hbm_out, scaled_hbm, delta_hbm, mine_hbm, other_hbm, query_hbm, parts_hbm = rest[:8]
    queries, lse, lat_grad, lat_scaled, delta = rest[8:13]
    out_grad, saved, value_up, lat_ref, pos_ref, grad_s, saved_s, part_s, parts, key_s = rest[-16:-6]
    key_own, key_mine, key_other, query_own, sem, out_sem = rest[-6:]
    side = lax.rem(lax.axis_index("ctx"), 2)
    core = lax.rem(lax.axis_index("head"), 2)
    moves = [
        (out_grad_hbm, out_grad),
        (saved_hbm, saved),
        (up_hbm, value_up),
        (q_hbm, queries),
        (lat_hbm, lat_ref),
        (pos_hbm, pos_ref),
        (lse_hbm, lse),
    ]
    copies = [pltpu.make_async_copy(src, dst, sem.at[i]) for i, (src, dst) in enumerate(moves)]
    for copy in copies:
        copy.start()
    heads = queries.shape[0]
    n_ctx, n_dp = part_s.shape[:2]
    width = LATENT // (n_ctx * n_dp)
    copies[0].wait()
    grad_s[...] = out_grad[...].astype(F32)
    copies[1].wait()
    saved_s[0] = saved[:, :VHEAD].astype(F32)
    saved_s[1] = saved[:, VHEAD:].astype(F32)
    for copy in copies[2:]:
        copy.wait()

    def one(h, _):
        grad_h = grad_s[pl.ds(h, TOK, stride=heads), :].astype(BF16)
        saved_h = jnp.concatenate([saved_s[c, pl.ds(h, TOK, stride=heads), :].T for c in range(2)], axis=0)
        lat = dot_nt(value_up[h], grad_h)
        scaled = (lat * SCALING).astype(BF16)
        lat_grad[h] = lat.astype(BF16)
        lat_scaled[h] = scaled
        delta[pl.ds(h, 1), :] = jnp.sum(scaled.astype(F32) * saved_h, axis=0, keepdims=True)
        part = dot(saved_h.astype(BF16), grad_h)
        for d in range(n_dp):
            rows = part[d * n_ctx * width : (d + 1) * n_ctx * width]
            part_s[:, d, pl.ds(width * h, width), :] = rows.reshape(n_ctx, width, VHEAD)
        return 0

    lax.fori_loop(0, heads, one, 0, unroll=4)
    start[...] = jnp.zeros_like(start)
    outs = [
        (parts, parts_hbm),
        (lat_grad, lat_hbm_out),
        (lat_scaled, scaled_hbm),
        (delta, delta_hbm),
        (key_mine, mine_hbm),
        (key_other, other_hbm),
        (query_own, query_hbm),
    ]
    outs = [pltpu.make_async_copy(src, dst, out_sem.at[i]) for i, (src, dst) in enumerate(outs)]
    parts[...] = part_s[...].astype(BF16)
    for copy in outs[:4]:
        copy.start()

    key_s[...] = lat_ref[...].T
    pos_q = pos_ref[...].astype(F32)
    pos_k = jnp.broadcast_to(pos_q, (TOK, TOK)).T
    visible = pos_k <= jnp.broadcast_to(pos_q, (TOK, TOK))
    visible = jnp.concatenate([visible, visible], axis=1)
    key_own[...] = jnp.zeros_like(key_own)
    for pair in range(heads // 2):
        q2 = both(queries, pair)
        logits = dot(key_s[...], q2)
        weights = jnp.where(visible, jnp.exp2(logits * (SCALING * LOG2E) - both_rows(lse, pair) * LOG2E), 0.0)
        dot_value = dot(key_s[:, :LATENT], both(lat_scaled, pair))
        dl = (weights * (dot_value - both_rows(delta, pair))).astype(BF16)
        query_own[pair] = dot(lat_ref[...], dl)
        key_own[...] += dot_nt(q2, dl)
        key_own[:LATENT] += dot_nt(both(lat_grad, pair), weights.astype(BF16))
    here = lax.broadcasted_iota(jnp.int32, (FULL, TOK), 1) // HALF == side
    own = key_own[...]
    kept = jnp.where(here, own, 0.0)
    moved = jnp.where(here, jnp.concatenate([own[:, HALF:], own[:, :HALF]], axis=1), 0.0)
    key_mine[...] = jnp.where(core == side, kept, moved)
    key_other[...] = jnp.where(core == side, moved, kept)
    for copy in outs[4:]:
        copy.start()
    for copy in outs:
        copy.wait()


def attention_kernel(
    first, last, recv_hbm, pos_hbm, q_hbm, lse_hbm, lat_hbm, scaled_hbm, delta_hbm, own_hbm, so_far, after,
    query_hbm, key_out, done,
    recv, pos, queries, lse, lat_grad, lat_scaled, delta, key_own, key_acc, key_s, keys_t, query_s, last_s, sem, in_sem,
):
    heads = queries.shape[0]
    count = key_s.shape[0] // HALF
    quarter = max(1, count // 4)
    base = count // quarter
    moves = []
    for lo in range(0, count, quarter):
        moves.append((recv_hbm.at[first + lo : first + lo + quarter], recv.at[lo : lo + quarter]))
    moves += [(lse_hbm, lse), (delta_hbm, delta), (pos_hbm, pos)]
    near = heads // 4
    for lo in range(0, heads, near):
        pieces = ((q_hbm, queries), (scaled_hbm, lat_scaled), (lat_hbm, lat_grad))
        moves += [(src.at[lo : lo + near], dst.at[lo : lo + near]) for src, dst in pieces]
        moves.append((so_far.at[lo // 2 : (lo + near) // 2], query_s.at[lo // 2 : (lo + near) // 2]))
    moves.append((own_hbm, key_own))
    copies = [pltpu.make_async_copy(src, dst, in_sem.at[i]) for i, (src, dst) in enumerate(moves)]
    for copy in copies:
        copy.start()
    own = lax.axis_index("ctx")
    key_acc[...] = jnp.zeros_like(key_acc)
    for j in range(count):
        if j % quarter == 0:
            copies[j // quarter].wait()
        lo = HALF * j
        key_s[lo : lo + HALF, :TOK] = recv[j, :HALF]
        key_s[lo : lo + HALF, TOK:LATENT] = recv[j, HALF:ROT]
        rot = recv[j, ROT:RANK].astype(F32)
        for g in range(HALF // 16):
            key_s[lo + 16 * g : lo + 16 * g + 16, LATENT:] = rot[:, ROPE * g : ROPE * g + ROPE].astype(BF16)
    copies[base + 2].wait()
    rank_q = jnp.min(pos[...].astype(F32), axis=1, keepdims=True) * (1.0 / TOK)
    far = []
    for j in range(count):
        one_far = jnp.where(recv[j, RANK : RANK + 1, :].astype(F32) < rank_q, 0.0, FAR)
        far.append(jnp.concatenate([one_far, one_far], axis=1))
    def copy_out(pair):
        if last:
            part = pl.ds(2 * pair, 2)
            return pltpu.make_async_copy(last_s.at[part], query_hbm.at[part], sem.at[pair])
        return pltpu.make_async_copy(query_s.at[pair], query_hbm.at[pair], sem.at[pair])

    def one(pair, _):
        q2 = both(queries, pair)
        logits = dot(key_s[...], q2)
        dot_value = dot(key_s[:, :LATENT], both(lat_scaled, pair))
        lse2 = both_rows(lse, pair) * LOG2E
        delta2 = both_rows(delta, pair)
        weights = jnp.concatenate(
            [
                jnp.exp2(logits[HALF * j : HALF * j + HALF] * (SCALING * LOG2E) - (lse2 + far[j]))
                for j in range(count)
            ],
            axis=0,
        )
        dl = (weights * (dot_value - delta2)).astype(BF16)
        grad = query_s[pair] + dot(keys_t[...], dl)
        if last:
            last_s[2 * pair] = grad[:, :TOK].astype(BF16)
            last_s[2 * pair + 1] = grad[:, TOK:].astype(BF16)
        else:
            query_s[pair] = grad
        copy_out(pair).start()
        key_acc[:LATENT] += dot_nt(
            jnp.concatenate([q2[:LATENT], both(lat_grad, pair)], axis=1),
            jnp.concatenate([dl, weights.astype(BF16)], axis=1),
        )
        key_acc[LATENT:] += dot_nt(q2[LATENT:], dl)
        return 0

    for i in range(4):
        at = base + 3 + 4 * i
        for copy in copies[at : at + 4] if i else copies[base : base + 2] + copies[at : at + 4]:
            copy.wait()
        if i == 0:
            for lo in range(0, count * HALF, TOK):
                keys_t[:, lo : lo + TOK] = key_s[lo : lo + TOK, :].T
        lax.fori_loop(near // 2 * i, near // 2 * (i + 1), one, 0, unroll=near // 2)
    copies[-1].wait()
    for t in range(count * HALF // TOK):
        total = key_acc[:, TOK * t : TOK * t + TOK]
        total = total + jnp.where(own // 2 == first // 2 + t, 1.0, 0.0) * key_own[...]
        key_out[:, TOK * t : TOK * t + TOK] = total.astype(key_out.dtype)
    done[...] = after[: done.shape[0]]
    for pair in range(heads // 2):
        copy_out(pair).wait()


def pack_kernel(mine_1, mine_2, recv, after, out_ref):
    del after
    t = 0
    for ref in (mine_1, mine_2):
        for i in range(ref.shape[1] // TOK):
            tile = ref[:, TOK * i : TOK * i + TOK] + recv[:, TOK * t : TOK * t + TOK].astype(F32)
            low, high = tile[:SPLIT], tile[SPLIT:]
            out_ref[2 * t] = jnp.concatenate([low[:, :HALF], high[:, :HALF]], axis=1).astype(BF16)
            out_ref[2 * t + 1] = jnp.concatenate([low[:, HALF:], high[:, HALF:]], axis=1).astype(BF16)
            t += 1


def weight_kernel(recv, after, friend_ref, keep_ref):
    del after
    total = recv[0].astype(F32)
    for j in range(1, recv.shape[0]):
        total = total + recv[j].astype(F32)
    dp = lax.axis_index("dp")
    friend = dp + 1 - 2 * lax.rem(dp, 2)
    for ref, index in ((friend_ref, friend), (keep_ref, dp)):
        for i, part in enumerate((index, recv.shape[1] - 1 - index)):
            chosen = total[0]
            for d in range(1, recv.shape[1]):
                chosen = jnp.where(part == d, total[d], chosen)
            ref[i] = chosen.astype(BF16)


def middle_kernel(keep, recv, stay_ref, send_ref):
    total = keep[...].astype(F32) + recv[...].astype(F32)
    stay_ref[...] = total[0]
    send_ref[...] = total[1].astype(BF16)


def sum_kernel(recv, key_ref):
    total = recv[0].astype(F32)
    for j in range(1, recv.shape[0]):
        total = total + recv[j].astype(F32)
    key_ref[...] = total.astype(BF16)


def share_kernel(stay, weight_recv, after, weight_ref, part_s):
    del after
    part_s[...] = stay[...] + weight_recv[...].astype(F32)
    width, heads = weight_ref.shape[0], weight_ref.shape[1]
    for i in range(width):
        weight_ref[i] = part_s[pl.ds(i, heads, stride=width), :]


def last_kernel(parts, out_ref):
    sides = []
    for core in range(2):
        total = parts[core].astype(F32)
        for other in range(core + 2, parts.shape[0], 2):
            total = total + parts[other].astype(F32)
        sides.append(total)
    out_ref[:SPLIT] = jnp.concatenate([sides[0][:, :HALF], sides[1][:, :HALF]], axis=1)
    out_ref[SPLIT:] = jnp.concatenate([sides[0][:, HALF:], sides[1][:, HALF:]], axis=1)


def body(queries, latents, positions, lse, saved_out, out_grad, value_up):
    n_dp, n_ctx, n_head = lax.axis_size("dp"), lax.axis_size("ctx"), lax.axis_size("head")
    heads = queries.shape[2]
    groups = n_dp * n_ctx
    width = LATENT // groups
    pairs = heads // 2
    q_t = far_away(jnp.transpose(queries[0], (1, 2, 0)))
    lat_t = far_away(latents[0].T)
    lse_t = far_away(lse[0].T)
    positions = far_away(positions)
    def core_swap(x):
        return lax.ppermute(x, "head", [(i, i ^ 1) for i in range(n_head)])

    payload = pl.pallas_call(
        payload_kernel,
        out_shape=shape((n_ctx, BLOCK, TOK), BF16),
        in_specs=[ANY, ANY],
        out_specs=ANY,
        scratch_shapes=[
            pltpu.VMEM((BLOCK, TOK), BF16),
            pltpu.VMEM((FULL, TOK), BF16),
            pltpu.VMEM((TOK, FULL), BF16),
            pltpu.VMEM((1, TOK), jnp.int32),
            pltpu.SemaphoreType.DMA((2,)),
            pltpu.SemaphoreType.DMA((n_ctx,)),
        ],
        compiler_params=vmem(2),
    )(lat_t, positions)
    recv_mine = lax.all_to_all(payload, "ctx", 0, 0)

    part_rows = heads * width
    start, lat_grad, lat_scaled, delta, key_mine, key_other, query_own, parts = pl.pallas_call(
        prologue_kernel,
        out_shape=[
            near_shape((8, TOK), F32),
            far_shape((heads, LATENT, TOK), BF16),
            far_shape((heads, LATENT, TOK), BF16),
            far_shape((heads, TOK), F32),
            far_shape((FULL, TOK), F32),
            far_shape((FULL, TOK), F32),
            far_shape((pairs, FULL, 2 * TOK), F32),
            far_shape((n_ctx, n_dp, part_rows, VHEAD), BF16),
        ],
        in_specs=[ANY] * 7,
        out_specs=[VM] + [ANY] * 7,
        scratch_shapes=[
            pltpu.VMEM((heads, FULL, TOK), BF16),
            pltpu.VMEM((heads, TOK), F32),
            pltpu.VMEM((heads, LATENT, TOK), BF16),
            pltpu.VMEM((heads, LATENT, TOK), BF16),
            pltpu.VMEM((heads, TOK), F32),
            pltpu.VMEM((TOK * heads, VHEAD), BF16),
            pltpu.VMEM((TOK * heads, LATENT), BF16),
            pltpu.VMEM((heads, LATENT, VHEAD), BF16),
            pltpu.VMEM((FULL, TOK), BF16),
            pltpu.VMEM((1, TOK), jnp.int32),
            pltpu.VMEM((TOK * heads, VHEAD), F32),
            pltpu.VMEM((2, TOK * heads, VHEAD), F32),
            pltpu.VMEM((n_ctx, n_dp, part_rows, VHEAD), F32),
            pltpu.VMEM((n_ctx, n_dp, part_rows, VHEAD), BF16),
            pltpu.VMEM((TOK, FULL), BF16),
            pltpu.VMEM((FULL, TOK), F32),
            pltpu.VMEM((FULL, TOK), F32),
            pltpu.VMEM((FULL, TOK), F32),
            pltpu.VMEM((pairs, FULL, 2 * TOK), F32),
            pltpu.SemaphoreType.DMA((7,)),
            pltpu.SemaphoreType.DMA((7,)),
        ],
        compiler_params=vmem(28),
        cost_estimate=cost(2 * heads * TOK * TOK * 1900, 8 << 20, heads * TOK * TOK),
    )(
        far_away(out_grad[0].reshape(TOK * heads, VHEAD)),
        far_away(saved_out[0].reshape(TOK * heads, LATENT)),
        far_away(value_up),
        q_t,
        lat_t,
        positions,
        lse_t,
    )
    recv_other = core_swap(recv_mine)

    def attend(recv, first, count, other, last, so_far, after):
        rows = count * HALF
        return pl.pallas_call(
            functools.partial(attention_kernel, first, last),
            out_shape=[
                shape((heads, FULL, TOK), BF16) if last else far_shape((pairs, FULL, 2 * TOK), F32),
                shape((FULL, rows), BF16) if other else near_shape((FULL, rows), F32),
                near_shape((8, TOK), F32),
            ],
            in_specs=[ANY] * 9 + [VM],
            out_specs=[ANY, VM, VM],
            scratch_shapes=[
                pltpu.VMEM((count, BLOCK, TOK), BF16),
                pltpu.VMEM((1, TOK), jnp.int32),
                pltpu.VMEM((heads, FULL, TOK), BF16),
                pltpu.VMEM((heads, TOK), F32),
                pltpu.VMEM((heads, LATENT, TOK), BF16),
                pltpu.VMEM((heads, LATENT, TOK), BF16),
                pltpu.VMEM((heads, TOK), F32),
                pltpu.VMEM((FULL, TOK), F32),
                pltpu.VMEM((FULL, rows), F32),
                pltpu.VMEM((rows, FULL), BF16),
                pltpu.VMEM((FULL, rows), BF16),
                pltpu.VMEM((pairs, FULL, 2 * TOK), F32),
                pltpu.VMEM((heads, FULL, TOK), BF16),
                pltpu.SemaphoreType.DMA((pairs,)),
                pltpu.SemaphoreType.DMA((24,)),
            ],
            compiler_params=vmem(24),
            cost_estimate=cost(1 << 33, 1 << 16),
        )(
            recv, positions, q_t, lse_t, far_away(lat_grad), far_away(lat_scaled), far_away(delta),
            far_away(key_other if other else key_mine), far_away(so_far), held(after),
        )

    near = n_ctx // 2
    query, sum_1, step = attend(recv_mine, 0, near, False, False, query_own, start)
    query, sum_2, step = attend(recv_other, 0, n_ctx, True, False, query, step)
    sum_recv = core_swap(sum_2)
    query_grad, sum_3, step = attend(recv_mine, near, n_ctx - near, False, True, query, step)

    weight_ctx = lax.all_to_all(parts, "ctx", 0, 0)
    packed = pl.pallas_call(
        pack_kernel,
        out_shape=shape((n_ctx, SPLIT, TOK), BF16),
        in_specs=[VM] * 3 + [ANY],
        out_specs=VM,
        compiler_params=vmem(6),
    )(held(sum_1), held(sum_3), sum_recv, weight_ctx)
    summed = lax.all_to_all(packed, "ctx", 0, 0)

    send_1, keep_1 = pl.pallas_call(
        weight_kernel,
        out_shape=[
            shape((2, part_rows, VHEAD), BF16),
            shape((2, part_rows, VHEAD), BF16),
        ],
        in_specs=[VM, ANY],
        out_specs=[VM] * 2,
        compiler_params=vmem(4),
        cost_estimate=cost(1 << 16, 1 << 16),
    )(weight_ctx, packed)

    recv_1 = lax.ppermute(send_1, "dp", [(i, i ^ 1) for i in range(n_dp)])
    stay, send_2 = pl.pallas_call(
        middle_kernel,
        out_shape=[shape((part_rows, VHEAD), F32), shape((part_rows, VHEAD), BF16)],
        in_specs=[VM] * 2,
        out_specs=[VM] * 2,
        compiler_params=vmem(2),
        cost_estimate=cost(1 << 16, 1 << 16),
    )(keep_1, recv_1)
    recv_2 = lax.ppermute(send_2, "dp", [(i, n_dp - 1 - i) for i in range(n_dp)])
    key_part = pl.pallas_call(
        sum_kernel,
        out_shape=shape((SPLIT, TOK), BF16),
        in_specs=[VM],
        out_specs=VM,
        compiler_params=vmem(4),
    )(summed)
    weight_share = pl.pallas_call(
        share_kernel,
        out_shape=shape((width, heads, VHEAD), F32),
        in_specs=[VM] * 2 + [ANY],
        out_specs=VM,
        scratch_shapes=[pltpu.VMEM((heads * width, VHEAD), F32)],
        compiler_params=vmem(2),
        cost_estimate=cost(1 << 16, 1 << 16),
    )(stay, recv_2, key_part)
    key_grad = pl.pallas_call(
        last_kernel,
        out_shape=shape((FULL, TOK), F32),
        in_specs=[VM],
        out_specs=VM,
        compiler_params=vmem(2),
    )(lax.all_gather(key_part, "head"))
    return (jnp.transpose(query_grad, (2, 0, 1))[None], key_grad.T[None], weight_share)


def solution(mesh):
    return jax.shard_map(
        body,
        mesh=mesh,
        in_specs=(
            P("dp", "ctx", "head", None),
            P("dp", "ctx", None),
            P("dp", "ctx"),
            P("dp", "ctx", "head"),
            P("dp", "ctx", "head", None),
            P("dp", "ctx", "head", None),
            P("head", None, None),
        ),
        out_specs=(
            P("dp", "ctx", "head", None),
            P("dp", "ctx", None),
            P(("dp", "ctx"), "head", None),
        ),
        check_vma=False,
    )
```

```python
import functools

import jax
import jax.numpy as jnp
from jax import lax
from jax.experimental import pallas as pl
from jax.experimental.pallas import tpu as pltpu
from jax.sharding import PartitionSpec as P

ROPE = 32
VHEAD = 128
LATENT = 256
FULL = LATENT + ROPE
TOK = 128
HALF = TOK // 2
SCALING = (VHEAD + ROPE) ** -0.5
LOG2E = 1.4426950408889634
FAR = 1e30
ROT = 2 * HALF
RANK = ROT + HALF * ROPE // TOK
BLOCK = RANK + 16
SPLIT = FULL // 2
F32 = jnp.float32
BF16 = jnp.bfloat16
NT = (((1,), (1,)), ((), ()))
VM = pl.BlockSpec(memory_space=pltpu.VMEM)
ANY = pl.BlockSpec(memory_space=pl.ANY)
SM = pl.BlockSpec(memory_space=pltpu.SMEM)


def vmem(mib):
    return pltpu.CompilerParams(vmem_limit_bytes=mib << 20)


def cost(flops, nbytes, exps=0):
    return pl.CostEstimate(flops=flops, bytes_accessed=nbytes, transcendentals=exps)


def shape(dims, dtype):
    return jax.ShapeDtypeStruct(dims, dtype)


def near_shape(dims, dtype):
    return pltpu.VMEM(dims, dtype)


def far_shape(dims, dtype):
    return pltpu.HBM(dims, dtype)


def held(x):
    return pltpu.with_memory_space_constraint(x, pltpu.VMEM)


def far_away(x):
    return pltpu.with_memory_space_constraint(x, pltpu.HBM)


def dot(a, b):
    return jnp.dot(a, b, preferred_element_type=F32)


def dot_nt(a, b):
    return lax.dot_general(a, b, NT, preferred_element_type=F32)


def both(ref, pair):
    return jnp.concatenate([ref[2 * pair], ref[2 * pair + 1]], axis=1)


def both_rows(ref, pair):
    return jnp.concatenate([ref[pl.ds(2 * pair, 1), :], ref[pl.ds(2 * pair + 1, 1), :]], axis=1)


def payload_kernel(lat_hbm, pos_hbm, out_hbm, block, lat_s, key_s, pos_s, in_sem, out_sem):
    lat_in = pltpu.make_async_copy(lat_hbm, lat_s, in_sem.at[0])
    pos_in = pltpu.make_async_copy(pos_hbm, pos_s, in_sem.at[1])
    lat_in.start()
    pos_in.start()
    pos_in.wait()
    base = jnp.min(pos_s[...].astype(F32), axis=1, keepdims=True)
    block[RANK:] = jnp.broadcast_to(base * (1.0 / TOK), (BLOCK - RANK, TOK)).astype(BF16)
    lat_in.wait()
    key_s[...] = lat_s[...].T
    half = key_s[pl.ds(pl.multiple_of(lax.rem(lax.axis_index("head"), 2) * HALF, HALF), HALF), :]
    block[:HALF] = half[:, :TOK]
    block[HALF:ROT] = half[:, TOK:LATENT]
    rot = half[:, LATENT:].astype(F32)
    block[ROT:RANK] = jnp.concatenate([rot[16 * g : 16 * g + 16] for g in range(HALF // 16)], axis=1).astype(BF16)
    copies = [pltpu.make_async_copy(block, out_hbm.at[j], out_sem.at[j]) for j in range(out_hbm.shape[0])]
    for copy in copies:
        copy.start()
    for copy in copies:
        copy.wait()


def prologue_kernel(out_grad_hbm, saved_hbm, up_hbm, q_hbm, lat_hbm, pos_hbm, lse_hbm, *rest):
    start, lat_hbm_out, scaled_hbm, delta_hbm, mine_hbm, other_hbm, query_hbm, parts_hbm = rest[:8]
    queries, lse, lat_grad, lat_scaled, delta = rest[8:13]
    out_grad, saved, value_up, lat_ref, pos_ref, grad_s, saved_s, part_s, parts, key_s = rest[-16:-6]
    key_own, key_mine, key_other, query_own, sem, out_sem = rest[-6:]
    side = lax.rem(lax.axis_index("ctx"), 2)
    core = lax.rem(lax.axis_index("head"), 2)
    moves = [
        (out_grad_hbm, out_grad),
        (saved_hbm, saved),
        (up_hbm, value_up),
        (q_hbm, queries),
        (lat_hbm, lat_ref),
        (pos_hbm, pos_ref),
        (lse_hbm, lse),
    ]
    copies = [pltpu.make_async_copy(src, dst, sem.at[i]) for i, (src, dst) in enumerate(moves)]
    for copy in copies:
        copy.start()
    heads = queries.shape[0]
    n_ctx, n_dp = part_s.shape[:2]
    width = LATENT // (n_ctx * n_dp)
    copies[0].wait()
    grad_s[...] = out_grad[...].astype(F32)
    copies[1].wait()
    saved_s[0] = saved[:, :VHEAD].astype(F32)
    saved_s[1] = saved[:, VHEAD:].astype(F32)
    for copy in copies[2:]:
        copy.wait()

    def one(h, _):
        grad_h = grad_s[pl.ds(h, TOK, stride=heads), :].astype(BF16)
        saved_h = jnp.concatenate([saved_s[c, pl.ds(h, TOK, stride=heads), :].T for c in range(2)], axis=0)
        lat = dot_nt(value_up[h], grad_h)
        scaled = (lat * SCALING).astype(BF16)
        lat_grad[h] = lat.astype(BF16)
        lat_scaled[h] = scaled
        delta[pl.ds(h, 1), :] = jnp.sum(scaled.astype(F32) * saved_h, axis=0, keepdims=True)
        part = dot(saved_h.astype(BF16), grad_h)
        for d in range(n_dp):
            rows = part[d * n_ctx * width : (d + 1) * n_ctx * width]
            part_s[:, d, pl.ds(width * h, width), :] = rows.reshape(n_ctx, width, VHEAD)
        return 0

    lax.fori_loop(0, heads, one, 0, unroll=4)
    start[...] = jnp.zeros_like(start)
    outs = [
        (parts, parts_hbm),
        (lat_grad, lat_hbm_out),
        (lat_scaled, scaled_hbm),
        (delta, delta_hbm),
        (key_mine, mine_hbm),
        (key_other, other_hbm),
        (query_own, query_hbm),
    ]
    outs = [pltpu.make_async_copy(src, dst, out_sem.at[i]) for i, (src, dst) in enumerate(outs)]
    parts[...] = part_s[...].astype(BF16)
    for copy in outs[:4]:
        copy.start()

    key_s[...] = lat_ref[...].T
    pos_q = pos_ref[...].astype(F32)
    pos_k = jnp.broadcast_to(pos_q, (TOK, TOK)).T
    visible = pos_k <= jnp.broadcast_to(pos_q, (TOK, TOK))
    visible = jnp.concatenate([visible, visible], axis=1)
    key_own[...] = jnp.zeros_like(key_own)
    for pair in range(heads // 2):
        q2 = both(queries, pair)
        logits = dot(key_s[...], q2)
        weights = jnp.where(visible, jnp.exp2(logits * (SCALING * LOG2E) - both_rows(lse, pair) * LOG2E), 0.0)
        dot_value = dot(key_s[:, :LATENT], both(lat_scaled, pair))
        dl = (weights * (dot_value - both_rows(delta, pair))).astype(BF16)
        query_own[pair] = dot(lat_ref[...], dl)
        key_own[...] += dot_nt(q2, dl)
        key_own[:LATENT] += dot_nt(both(lat_grad, pair), weights.astype(BF16))
    here = lax.broadcasted_iota(jnp.int32, (FULL, TOK), 1) // HALF == side
    own = key_own[...]
    kept = jnp.where(here, own, 0.0)
    moved = jnp.where(here, jnp.concatenate([own[:, HALF:], own[:, :HALF]], axis=1), 0.0)
    key_mine[...] = jnp.where(core == side, kept, moved)
    key_other[...] = jnp.where(core == side, moved, kept)
    for copy in outs[4:]:
        copy.start()
    for copy in outs:
        copy.wait()


def attention_kernel(first, last, stage, *rest):
    recv_hbm, pos_hbm, *operands, own_hbm, so_far, after = rest[:10]
    query_out, key_out, done = rest[10:13]
    recv, pos, key_own, key_acc, key_s, keys_t, last_s, sem, in_sem = rest[-9:]
    queries, lse, lat_grad, lat_scaled, delta = rest[13:18] if stage else operands
    heads = queries.shape[0]
    count = key_s.shape[0] // HALF
    quarter = max(1, count // 4)
    copies = []

    def fetch(src, dst):
        copies.append(pltpu.make_async_copy(src, dst, in_sem.at[len(copies)]))
        copies[-1].start()
        return copies[-1]

    key_copies = [
        fetch(recv_hbm.at[first + lo : first + lo + quarter], recv.at[lo : lo + quarter])
        for lo in range(0, count, quarter)
    ]
    pos_copy = fetch(pos_hbm, pos)
    near = heads // 4
    groups = [[fetch(operands[1], lse), fetch(operands[4], delta)] if stage else []] + [[], [], []]
    for i in range(4):
        part = slice(near * i, near * i + near)
        if stage:
            groups[i] += [
                fetch(src.at[part], dst.at[part])
                for src, dst in ((operands[0], queries), (operands[3], lat_scaled), (operands[2], lat_grad))
            ]
            half = slice(near // 2 * i, near // 2 * (i + 1))
            groups[i].append(fetch(so_far.at[half], query_out.at[half]))
    own_copy = fetch(own_hbm, key_own)
    own = lax.axis_index("ctx")
    key_acc[...] = jnp.zeros_like(key_acc)
    for j in range(count):
        if j % quarter == 0:
            key_copies[j // quarter].wait()
        lo = HALF * j
        key_s[lo : lo + HALF, :TOK] = recv[j, :HALF]
        key_s[lo : lo + HALF, TOK:LATENT] = recv[j, HALF:ROT]
        rot = recv[j, ROT:RANK].astype(F32)
        for g in range(HALF // 16):
            key_s[lo + 16 * g : lo + 16 * g + 16, LATENT:] = rot[:, ROPE * g : ROPE * g + ROPE].astype(BF16)
    pos_copy.wait()
    rank_q = jnp.min(pos[...].astype(F32), axis=1, keepdims=True) * (1.0 / TOK)
    far = []
    for j in range(count):
        one_far = jnp.where(recv[j, RANK : RANK + 1, :].astype(F32) < rank_q, 0.0, FAR)
        far.append(jnp.concatenate([one_far, one_far], axis=1))
    def copy_out(pair):
        part = pl.ds(2 * pair, 2)
        return pltpu.make_async_copy(last_s.at[part], query_out.at[part], sem.at[pair])

    def one(pair, _):
        q2 = both(queries, pair)
        logits = dot(key_s[...], q2)
        dot_value = dot(key_s[:, :LATENT], both(lat_scaled, pair))
        lse2 = both_rows(lse, pair) * LOG2E
        delta2 = both_rows(delta, pair)
        weights = jnp.concatenate(
            [
                jnp.exp2(logits[HALF * j : HALF * j + HALF] * (SCALING * LOG2E) - (lse2 + far[j]))
                for j in range(count)
            ],
            axis=0,
        )
        dl = (weights * (dot_value - delta2)).astype(BF16)
        grad = (query_out if stage else so_far)[pair] + dot(keys_t[...], dl)
        if last:
            last_s[2 * pair] = grad[:, :TOK].astype(BF16)
            last_s[2 * pair + 1] = grad[:, TOK:].astype(BF16)
            copy_out(pair).start()
        else:
            query_out[pair] = grad
        key_acc[:LATENT] += dot_nt(
            jnp.concatenate([q2[:LATENT], both(lat_grad, pair)], axis=1),
            jnp.concatenate([dl, weights.astype(BF16)], axis=1),
        )
        key_acc[LATENT:] += dot_nt(q2[LATENT:], dl)
        return 0

    for lo in range(0, count * HALF, TOK):
        keys_t[:, lo : lo + TOK] = key_s[lo : lo + TOK, :].T
    steps = 4 if stage else 1
    for i in range(steps):
        for copy in groups[i]:
            copy.wait()
        each = heads // 2 // steps
        lax.fori_loop(each * i, each * i + each, one, 0, unroll=each)
    own_copy.wait()
    for t in range(count * HALF // TOK):
        total = key_acc[:, TOK * t : TOK * t + TOK]
        total = total + jnp.where(own // 2 == first // 2 + t, 1.0, 0.0) * key_own[...]
        key_out[:, TOK * t : TOK * t + TOK] = total.astype(key_out.dtype)
    done[...] = after[: done.shape[0]]
    if last:
        for pair in range(heads // 2):
            copy_out(pair).wait()


def pack_kernel(mine_1, mine_2, recv, after, out_ref):
    del after
    t = 0
    for ref in (mine_1, mine_2):
        for i in range(ref.shape[1] // TOK):
            tile = ref[:, TOK * i : TOK * i + TOK] + recv[:, TOK * t : TOK * t + TOK].astype(F32)
            low, high = tile[:SPLIT], tile[SPLIT:]
            out_ref[2 * t] = jnp.concatenate([low[:, :HALF], high[:, :HALF]], axis=1).astype(BF16)
            out_ref[2 * t + 1] = jnp.concatenate([low[:, HALF:], high[:, HALF:]], axis=1).astype(BF16)
            t += 1


def weight_kernel(recv, after, friend_ref, keep_ref):
    del after
    total = recv[0].astype(F32)
    for j in range(1, recv.shape[0]):
        total = total + recv[j].astype(F32)
    dp = lax.axis_index("dp")
    friend = dp + 1 - 2 * lax.rem(dp, 2)
    for ref, index in ((friend_ref, friend), (keep_ref, dp)):
        for i, part in enumerate((index, recv.shape[1] - 1 - index)):
            chosen = total[0]
            for d in range(1, recv.shape[1]):
                chosen = jnp.where(part == d, total[d], chosen)
            ref[i] = chosen.astype(BF16)


def middle_kernel(keep, recv, stay_ref, send_ref):
    total = keep[...].astype(F32) + recv[...].astype(F32)
    stay_ref[...] = total[0]
    send_ref[...] = total[1].astype(BF16)


def sum_kernel(recv, key_ref):
    total = recv[0].astype(F32)
    for j in range(1, recv.shape[0]):
        total = total + recv[j].astype(F32)
    key_ref[...] = total.astype(BF16)


def share_kernel(stay, weight_recv, after, weight_ref, part_s):
    del after
    part_s[...] = stay[...] + weight_recv[...].astype(F32)
    width, heads = weight_ref.shape[0], weight_ref.shape[1]
    for i in range(width):
        weight_ref[i] = part_s[pl.ds(i, heads, stride=width), :]


def last_kernel(parts, out_ref):
    sides = []
    for core in range(2):
        total = parts[core].astype(F32)
        for other in range(core + 2, parts.shape[0], 2):
            total = total + parts[other].astype(F32)
        sides.append(total)
    out_ref[:SPLIT] = jnp.concatenate([sides[0][:, :HALF], sides[1][:, :HALF]], axis=1)
    out_ref[SPLIT:] = jnp.concatenate([sides[0][:, HALF:], sides[1][:, HALF:]], axis=1)


def body(queries, latents, positions, lse, saved_out, out_grad, value_up):
    n_dp, n_ctx, n_head = lax.axis_size("dp"), lax.axis_size("ctx"), lax.axis_size("head")
    heads = queries.shape[2]
    groups = n_dp * n_ctx
    width = LATENT // groups
    pairs = heads // 2
    q_t = far_away(jnp.transpose(queries[0], (1, 2, 0)))
    lat_t = far_away(latents[0].T)
    lse_t = far_away(lse[0].T)
    positions = far_away(positions)
    def core_swap(x):
        return lax.ppermute(x, "head", [(i, i ^ 1) for i in range(n_head)])

    payload = pl.pallas_call(
        payload_kernel,
        out_shape=shape((n_ctx, BLOCK, TOK), BF16),
        in_specs=[ANY, ANY],
        out_specs=ANY,
        scratch_shapes=[
            pltpu.VMEM((BLOCK, TOK), BF16),
            pltpu.VMEM((FULL, TOK), BF16),
            pltpu.VMEM((TOK, FULL), BF16),
            pltpu.VMEM((1, TOK), jnp.int32),
            pltpu.SemaphoreType.DMA((2,)),
            pltpu.SemaphoreType.DMA((n_ctx,)),
        ],
        compiler_params=vmem(2),
    )(lat_t, positions)
    recv_mine = lax.all_to_all(payload, "ctx", 0, 0)

    part_rows = heads * width
    start, lat_grad, lat_scaled, delta, key_mine, key_other, query_own, parts = pl.pallas_call(
        prologue_kernel,
        out_shape=[
            near_shape((8, TOK), F32),
            far_shape((heads, LATENT, TOK), BF16),
            far_shape((heads, LATENT, TOK), BF16),
            far_shape((heads, TOK), F32),
            far_shape((FULL, TOK), F32),
            far_shape((FULL, TOK), F32),
            far_shape((pairs, FULL, 2 * TOK), F32),
            far_shape((n_ctx, n_dp, part_rows, VHEAD), BF16),
        ],
        in_specs=[ANY] * 7,
        out_specs=[VM] + [ANY] * 7,
        scratch_shapes=[
            pltpu.VMEM((heads, FULL, TOK), BF16),
            pltpu.VMEM((heads, TOK), F32),
            pltpu.VMEM((heads, LATENT, TOK), BF16),
            pltpu.VMEM((heads, LATENT, TOK), BF16),
            pltpu.VMEM((heads, TOK), F32),
            pltpu.VMEM((TOK * heads, VHEAD), BF16),
            pltpu.VMEM((TOK * heads, LATENT), BF16),
            pltpu.VMEM((heads, LATENT, VHEAD), BF16),
            pltpu.VMEM((FULL, TOK), BF16),
            pltpu.VMEM((1, TOK), jnp.int32),
            pltpu.VMEM((TOK * heads, VHEAD), F32),
            pltpu.VMEM((2, TOK * heads, VHEAD), F32),
            pltpu.VMEM((n_ctx, n_dp, part_rows, VHEAD), F32),
            pltpu.VMEM((n_ctx, n_dp, part_rows, VHEAD), BF16),
            pltpu.VMEM((TOK, FULL), BF16),
            pltpu.VMEM((FULL, TOK), F32),
            pltpu.VMEM((FULL, TOK), F32),
            pltpu.VMEM((FULL, TOK), F32),
            pltpu.VMEM((pairs, FULL, 2 * TOK), F32),
            pltpu.SemaphoreType.DMA((7,)),
            pltpu.SemaphoreType.DMA((7,)),
        ],
        compiler_params=vmem(28),
        cost_estimate=cost(2 * heads * TOK * TOK * 1900, 8 << 20, heads * TOK * TOK),
    )(
        far_away(out_grad[0].reshape(TOK * heads, VHEAD)),
        far_away(saved_out[0].reshape(TOK * heads, LATENT)),
        far_away(value_up),
        q_t,
        lat_t,
        positions,
        lse_t,
    )
    recv_other = core_swap(recv_mine)

    held_shapes = [
        ((heads, FULL, TOK), BF16),
        ((heads, TOK), F32),
        ((heads, LATENT, TOK), BF16),
        ((heads, LATENT, TOK), BF16),
        ((heads, TOK), F32),
    ]

    def attend(recv, first, count, other, stage, last, operands, so_far, after):
        rows = count * HALF
        return pl.pallas_call(
            functools.partial(attention_kernel, first, last, stage),
            out_shape=[
                shape((heads, FULL, TOK), BF16) if last else near_shape((pairs, FULL, 2 * TOK), F32),
                shape((FULL, rows), BF16) if other else near_shape((FULL, rows), F32),
                near_shape((8, TOK), F32),
            ]
            + [near_shape(*h) for h in held_shapes if stage],
            in_specs=[ANY] * 2 + [ANY if stage else VM] * 5 + [ANY, ANY if stage else VM, VM],
            out_specs=[ANY if last else VM, VM, VM] + [VM] * (5 if stage else 0),
            scratch_shapes=[
                pltpu.VMEM((count, BLOCK, TOK), BF16),
                pltpu.VMEM((1, TOK), jnp.int32),
                pltpu.VMEM((FULL, TOK), F32),
                pltpu.VMEM((FULL, rows), F32),
                pltpu.VMEM((rows, FULL), BF16),
                pltpu.VMEM((FULL, rows), BF16),
                pltpu.VMEM((heads, FULL, TOK), BF16),
                pltpu.SemaphoreType.DMA((pairs,)),
                pltpu.SemaphoreType.DMA((24,)),
            ],
            input_output_aliases={} if stage or last else {8: 0},
            compiler_params=vmem(20),
            cost_estimate=cost(1 << 33, 1 << 16),
        )(
            recv, positions, *[far_away(x) if stage else held(x) for x in operands],
            far_away(key_other if other else key_mine), far_away(so_far) if stage else held(so_far), held(after),
        )

    near = n_ctx // 2
    query, sum_1, step, *staged = attend(
        recv_mine, 0, near, False, True, False, (q_t, lse_t, lat_grad, lat_scaled, delta), query_own, start
    )
    query, sum_2, step = attend(recv_other, 0, n_ctx, True, False, False, staged, query, step)
    sum_recv = core_swap(sum_2)
    query_grad, sum_3, step = attend(recv_mine, near, n_ctx - near, False, False, True, staged, query, step)

    weight_ctx = lax.all_to_all(parts, "ctx", 0, 0)
    packed = pl.pallas_call(
        pack_kernel,
        out_shape=shape((n_ctx, SPLIT, TOK), BF16),
        in_specs=[VM] * 3 + [ANY],
        out_specs=VM,
        compiler_params=vmem(6),
    )(held(sum_1), held(sum_3), sum_recv, weight_ctx)
    summed = lax.all_to_all(packed, "ctx", 0, 0)

    send_1, keep_1 = pl.pallas_call(
        weight_kernel,
        out_shape=[
            shape((2, part_rows, VHEAD), BF16),
            shape((2, part_rows, VHEAD), BF16),
        ],
        in_specs=[VM, ANY],
        out_specs=[VM] * 2,
        compiler_params=vmem(4),
        cost_estimate=cost(1 << 16, 1 << 16),
    )(weight_ctx, packed)

    recv_1 = lax.ppermute(send_1, "dp", [(i, i ^ 1) for i in range(n_dp)])
    stay, send_2 = pl.pallas_call(
        middle_kernel,
        out_shape=[shape((part_rows, VHEAD), F32), shape((part_rows, VHEAD), BF16)],
        in_specs=[VM] * 2,
        out_specs=[VM] * 2,
        compiler_params=vmem(2),
        cost_estimate=cost(1 << 16, 1 << 16),
    )(keep_1, recv_1)
    recv_2 = lax.ppermute(send_2, "dp", [(i, n_dp - 1 - i) for i in range(n_dp)])
    key_part = pl.pallas_call(
        sum_kernel,
        out_shape=shape((SPLIT, TOK), BF16),
        in_specs=[VM],
        out_specs=VM,
        compiler_params=vmem(4),
    )(summed)
    weight_share = pl.pallas_call(
        share_kernel,
        out_shape=shape((width, heads, VHEAD), F32),
        in_specs=[VM] * 2 + [ANY],
        out_specs=VM,
        scratch_shapes=[pltpu.VMEM((heads * width, VHEAD), F32)],
        compiler_params=vmem(2),
        cost_estimate=cost(1 << 16, 1 << 16),
    )(stay, recv_2, key_part)
    key_grad = pl.pallas_call(
        last_kernel,
        out_shape=shape((FULL, TOK), F32),
        in_specs=[VM],
        out_specs=VM,
        compiler_params=vmem(2),
    )(lax.all_gather(key_part, "head"))
    return (jnp.transpose(query_grad, (2, 0, 1))[None], key_grad.T[None], weight_share)


def solution(mesh):
    return jax.shard_map(
        body,
        mesh=mesh,
        in_specs=(
            P("dp", "ctx", "head", None),
            P("dp", "ctx", None),
            P("dp", "ctx"),
            P("dp", "ctx", "head"),
            P("dp", "ctx", "head", None),
            P("dp", "ctx", "head", None),
            P("head", None, None),
        ),
        out_specs=(
            P("dp", "ctx", "head", None),
            P("dp", "ctx", None),
            P(("dp", "ctx"), "head", None),
        ),
        check_vma=False,
    )
```

```python
import functools

import jax
import jax.numpy as jnp
from jax import lax
from jax.experimental import pallas as pl
from jax.experimental.pallas import tpu as pltpu
from jax.sharding import PartitionSpec as P

ROPE = 32
VHEAD = 128
LATENT = 256
FULL = LATENT + ROPE
TOK = 128
HALF = TOK // 2
SCALING = (VHEAD + ROPE) ** -0.5
LOG2E = 1.4426950408889634
FAR = 1e30
ROT = 2 * HALF
RANK = ROT + HALF * ROPE // TOK
BLOCK = RANK + 16
SPLIT = FULL // 2
F32 = jnp.float32
BF16 = jnp.bfloat16
NT = (((1,), (1,)), ((), ()))
VM = pl.BlockSpec(memory_space=pltpu.VMEM)
ANY = pl.BlockSpec(memory_space=pl.ANY)
SM = pl.BlockSpec(memory_space=pltpu.SMEM)


def vmem(mib):
    return pltpu.CompilerParams(vmem_limit_bytes=mib << 20)


def cost(flops, nbytes, exps=0):
    return pl.CostEstimate(flops=flops, bytes_accessed=nbytes, transcendentals=exps)


def shape(dims, dtype):
    return jax.ShapeDtypeStruct(dims, dtype)


def near_shape(dims, dtype):
    return pltpu.VMEM(dims, dtype)


def far_shape(dims, dtype):
    return pltpu.HBM(dims, dtype)


def held(x):
    return pltpu.with_memory_space_constraint(x, pltpu.VMEM)


def far_away(x):
    return pltpu.with_memory_space_constraint(x, pltpu.HBM)


def dot(a, b):
    return jnp.dot(a, b, preferred_element_type=F32)


def dot_nt(a, b):
    return lax.dot_general(a, b, NT, preferred_element_type=F32)


def both(ref, pair):
    return jnp.concatenate([ref[2 * pair], ref[2 * pair + 1]], axis=1)


def both_rows(ref, pair):
    return jnp.concatenate([ref[pl.ds(2 * pair, 1), :], ref[pl.ds(2 * pair + 1, 1), :]], axis=1)


def payload_kernel(lat_hbm, pos_hbm, out_hbm, block, lat_s, key_s, pos_s, in_sem, out_sem):
    lat_in = pltpu.make_async_copy(lat_hbm, lat_s, in_sem.at[0])
    pos_in = pltpu.make_async_copy(pos_hbm, pos_s, in_sem.at[1])
    lat_in.start()
    pos_in.start()
    pos_in.wait()
    base = jnp.min(pos_s[...].astype(F32), axis=1, keepdims=True)
    block[RANK:] = jnp.broadcast_to(base * (1.0 / TOK), (BLOCK - RANK, TOK)).astype(BF16)
    lat_in.wait()
    key_s[...] = lat_s[...].T
    half = key_s[pl.ds(pl.multiple_of(lax.rem(lax.axis_index("head"), 2) * HALF, HALF), HALF), :]
    block[:HALF] = half[:, :TOK]
    block[HALF:ROT] = half[:, TOK:LATENT]
    rot = half[:, LATENT:].astype(F32)
    block[ROT:RANK] = jnp.concatenate([rot[16 * g : 16 * g + 16] for g in range(HALF // 16)], axis=1).astype(BF16)
    copies = [pltpu.make_async_copy(block, out_hbm.at[j], out_sem.at[j]) for j in range(out_hbm.shape[0])]
    for copy in copies:
        copy.start()
    for copy in copies:
        copy.wait()


def prologue_kernel(out_grad_hbm, saved_hbm, up_hbm, q_hbm, lat_hbm, pos_hbm, lse_hbm, *rest):
    start, lat_hbm_out, scaled_hbm, delta_hbm, mine_hbm, other_hbm, query_hbm, parts_hbm = rest[:8]
    queries, lse, lat_grad, lat_scaled, delta = rest[8:13]
    out_grad, saved, value_up, lat_ref, pos_ref, grad_s, saved_s, part_s, parts, key_s = rest[-16:-6]
    key_own, key_mine, key_other, query_own, sem, out_sem = rest[-6:]
    side = lax.rem(lax.axis_index("ctx"), 2)
    core = lax.rem(lax.axis_index("head"), 2)
    moves = [
        (out_grad_hbm, out_grad),
        (saved_hbm, saved),
        (up_hbm, value_up),
        (q_hbm, queries),
        (lat_hbm, lat_ref),
        (pos_hbm, pos_ref),
        (lse_hbm, lse),
    ]
    copies = [pltpu.make_async_copy(src, dst, sem.at[i]) for i, (src, dst) in enumerate(moves)]
    for copy in copies:
        copy.start()
    heads = queries.shape[0]
    n_ctx, n_dp = part_s.shape[:2]
    width = LATENT // (n_ctx * n_dp)
    copies[0].wait()
    grad_s[...] = out_grad[...].astype(F32)
    copies[1].wait()
    saved_s[0] = saved[:, :VHEAD].astype(F32)
    saved_s[1] = saved[:, VHEAD:].astype(F32)
    for copy in copies[2:]:
        copy.wait()

    def one(h, _):
        grad_h = grad_s[pl.ds(h, TOK, stride=heads), :].astype(BF16)
        saved_h = jnp.concatenate([saved_s[c, pl.ds(h, TOK, stride=heads), :].T for c in range(2)], axis=0)
        lat = dot_nt(value_up[h], grad_h)
        scaled = (lat * SCALING).astype(BF16)
        lat_grad[h] = lat.astype(BF16)
        lat_scaled[h] = scaled
        delta[pl.ds(h, 1), :] = jnp.sum(scaled.astype(F32) * saved_h, axis=0, keepdims=True)
        part = dot(saved_h.astype(BF16), grad_h)
        for d in range(n_dp):
            rows = part[d * n_ctx * width : (d + 1) * n_ctx * width]
            part_s[:, d, pl.ds(width * h, width), :] = rows.reshape(n_ctx, width, VHEAD)
        return 0

    lax.fori_loop(0, heads, one, 0, unroll=4)
    start[...] = jnp.zeros_like(start)
    outs = [
        (parts, parts_hbm),
        (lat_grad, lat_hbm_out),
        (lat_scaled, scaled_hbm),
        (delta, delta_hbm),
        (key_mine, mine_hbm),
        (key_other, other_hbm),
        (query_own, query_hbm),
    ]
    outs = [pltpu.make_async_copy(src, dst, out_sem.at[i]) for i, (src, dst) in enumerate(outs)]
    parts[...] = part_s[...].astype(BF16)
    for copy in outs[:4]:
        copy.start()

    key_s[...] = lat_ref[...].T
    pos_q = pos_ref[...].astype(F32)
    pos_k = jnp.broadcast_to(pos_q, (TOK, TOK)).T
    visible = pos_k <= jnp.broadcast_to(pos_q, (TOK, TOK))
    visible = jnp.concatenate([visible, visible], axis=1)
    key_own[...] = jnp.zeros_like(key_own)
    for pair in range(heads // 2):
        q2 = both(queries, pair)
        logits = dot(key_s[...], q2)
        weights = jnp.where(visible, jnp.exp2(logits * (SCALING * LOG2E) - both_rows(lse, pair) * LOG2E), 0.0)
        dot_value = dot(key_s[:, :LATENT], both(lat_scaled, pair))
        dl = (weights * (dot_value - both_rows(delta, pair))).astype(BF16)
        query_own[pair] = dot(lat_ref[...], dl)
        key_own[...] += dot_nt(q2, dl)
        key_own[:LATENT] += dot_nt(both(lat_grad, pair), weights.astype(BF16))
    here = lax.broadcasted_iota(jnp.int32, (FULL, TOK), 1) // HALF == side
    own = key_own[...]
    kept = jnp.where(here, own, 0.0)
    moved = jnp.where(here, jnp.concatenate([own[:, HALF:], own[:, :HALF]], axis=1), 0.0)
    key_mine[...] = jnp.where(core == side, kept, moved)
    key_other[...] = jnp.where(core == side, moved, kept)
    for copy in outs[4:]:
        copy.start()
    for copy in outs:
        copy.wait()


def attention_kernel(first, last, stage, *rest):
    recv_hbm, pos_hbm, *operands, own_hbm, so_far, after = rest[:10]
    query_out, key_out, done = rest[10:13]
    recv, pos, key_own, key_acc, key_s, keys_t, last_s, sem, in_sem = rest[-9:]
    queries, lse, lat_grad, lat_scaled, delta = rest[13:18] if stage else operands
    heads = queries.shape[0]
    count = key_s.shape[0] // HALF
    quarter = max(1, count // 4)
    copies = []

    def fetch(src, dst):
        copies.append(pltpu.make_async_copy(src, dst, in_sem.at[len(copies)]))
        copies[-1].start()
        return copies[-1]

    key_copies = [
        fetch(recv_hbm.at[first + lo : first + lo + quarter], recv.at[lo : lo + quarter])
        for lo in range(0, count, quarter)
    ]
    pos_copy = fetch(pos_hbm, pos)
    near = heads // 4
    groups = [[fetch(operands[1], lse), fetch(operands[4], delta)] if stage else []] + [[], [], []]
    for i in range(4):
        part = slice(near * i, near * i + near)
        if stage:
            groups[i] += [
                fetch(src.at[part], dst.at[part])
                for src, dst in ((operands[0], queries), (operands[3], lat_scaled), (operands[2], lat_grad))
            ]
            half = slice(near // 2 * i, near // 2 * (i + 1))
            groups[i].append(fetch(so_far.at[half], query_out.at[half]))
    own_copy = fetch(own_hbm, key_own)
    own = lax.axis_index("ctx")
    key_acc[...] = jnp.zeros_like(key_acc)
    for j in range(count):
        if j % quarter == 0:
            key_copies[j // quarter].wait()
        lo = HALF * j
        key_s[lo : lo + HALF, :TOK] = recv[j, :HALF]
        key_s[lo : lo + HALF, TOK:LATENT] = recv[j, HALF:ROT]
        rot = recv[j, ROT:RANK].astype(F32)
        for g in range(HALF // 16):
            key_s[lo + 16 * g : lo + 16 * g + 16, LATENT:] = rot[:, ROPE * g : ROPE * g + ROPE].astype(BF16)
    pos_copy.wait()
    rank_q = jnp.min(pos[...].astype(F32), axis=1, keepdims=True) * (1.0 / TOK)
    far = []
    for j in range(count):
        one_far = jnp.where(recv[j, RANK : RANK + 1, :].astype(F32) < rank_q, 0.0, FAR)
        far.append(jnp.concatenate([one_far, one_far], axis=1))
    def copy_out(pair):
        part = pl.ds(2 * pair, 2)
        return pltpu.make_async_copy(last_s.at[part], query_out.at[part], sem.at[pair])

    def one(pair, _):
        q2 = both(queries, pair)
        logits = dot(key_s[...], q2)
        dot_value = dot(key_s[:, :LATENT], both(lat_scaled, pair))
        lse2 = both_rows(lse, pair) * LOG2E
        delta2 = both_rows(delta, pair)
        weights = jnp.concatenate(
            [
                jnp.exp2(logits[HALF * j : HALF * j + HALF] * (SCALING * LOG2E) - (lse2 + far[j]))
                for j in range(count)
            ],
            axis=0,
        )
        dl = (weights * (dot_value - delta2)).astype(BF16)
        grad = (query_out if stage else so_far)[pair] + dot(keys_t[...], dl)
        if last:
            last_s[2 * pair] = grad[:, :TOK].astype(BF16)
            last_s[2 * pair + 1] = grad[:, TOK:].astype(BF16)
            copy_out(pair).start()
        else:
            query_out[pair] = grad
        key_acc[:LATENT] += dot_nt(
            jnp.concatenate([q2[:LATENT], both(lat_grad, pair)], axis=1),
            jnp.concatenate([dl, weights.astype(BF16)], axis=1),
        )
        key_acc[LATENT:] += dot_nt(q2[LATENT:], dl)
        return 0

    for lo in range(0, count * HALF, TOK):
        keys_t[:, lo : lo + TOK] = key_s[lo : lo + TOK, :].T
    steps = 4 if stage else 1
    for i in range(steps):
        for copy in groups[i]:
            copy.wait()
        each = heads // 2 // steps
        lax.fori_loop(each * i, each * i + each, one, 0, unroll=each)
    own_copy.wait()
    for t in range(count * HALF // TOK):
        total = key_acc[:, TOK * t : TOK * t + TOK]
        total = total + jnp.where(own // 2 == first // 2 + t, 1.0, 0.0) * key_own[...]
        key_out[:, TOK * t : TOK * t + TOK] = total.astype(key_out.dtype)
    done[...] = after[: done.shape[0]]
    if last:
        for pair in range(heads // 2):
            copy_out(pair).wait()


def pack_kernel(mine_1, mine_2, recv, after, out_ref):
    del after
    t = 0
    for ref in (mine_1, mine_2):
        for i in range(ref.shape[1] // TOK):
            tile = ref[:, TOK * i : TOK * i + TOK] + recv[:, TOK * t : TOK * t + TOK].astype(F32)
            low, high = tile[:SPLIT], tile[SPLIT:]
            out_ref[2 * t] = jnp.concatenate([low[:, :HALF], high[:, :HALF]], axis=1).astype(BF16)
            out_ref[2 * t + 1] = jnp.concatenate([low[:, HALF:], high[:, HALF:]], axis=1).astype(BF16)
            t += 1


def weight_kernel(recv, after, friend_ref, keep_ref):
    del after
    total = recv[0].astype(F32)
    for j in range(1, recv.shape[0]):
        total = total + recv[j].astype(F32)
    dp = lax.axis_index("dp")
    friend = dp + 1 - 2 * lax.rem(dp, 2)
    for ref, index in ((friend_ref, friend), (keep_ref, dp)):
        for i, part in enumerate((index, recv.shape[1] - 1 - index)):
            chosen = total[0]
            for d in range(1, recv.shape[1]):
                chosen = jnp.where(part == d, total[d], chosen)
            ref[i] = chosen.astype(BF16)


def middle_kernel(keep, recv, stay_ref, send_ref):
    total = keep[...].astype(F32) + recv[...].astype(F32)
    stay_ref[...] = total[0]
    send_ref[...] = total[1].astype(BF16)


def sum_kernel(recv, key_ref):
    total = recv[0].astype(F32)
    for j in range(1, recv.shape[0]):
        total = total + recv[j].astype(F32)
    key_ref[...] = total.astype(BF16)


def last_kernel(parts, stay, weight_recv, out_ref, weight_ref, part_s):
    part_s[...] = stay[...] + weight_recv[...].astype(F32)
    width, heads = weight_ref.shape[0], weight_ref.shape[1]
    for i in range(width):
        weight_ref[i] = part_s[pl.ds(i, heads, stride=width), :]
    sides = []
    for core in range(2):
        total = parts[core].astype(F32)
        for other in range(core + 2, parts.shape[0], 2):
            total = total + parts[other].astype(F32)
        sides.append(total)
    out_ref[:SPLIT] = jnp.concatenate([sides[0][:, :HALF], sides[1][:, :HALF]], axis=1)
    out_ref[SPLIT:] = jnp.concatenate([sides[0][:, HALF:], sides[1][:, HALF:]], axis=1)


def body(queries, latents, positions, lse, saved_out, out_grad, value_up):
    n_dp, n_ctx, n_head = lax.axis_size("dp"), lax.axis_size("ctx"), lax.axis_size("head")
    heads = queries.shape[2]
    groups = n_dp * n_ctx
    width = LATENT // groups
    pairs = heads // 2
    q_t = far_away(jnp.transpose(queries[0], (1, 2, 0)))
    lat_t = far_away(latents[0].T)
    lse_t = far_away(lse[0].T)
    positions = far_away(positions)
    def core_swap(x):
        return lax.ppermute(x, "head", [(i, i ^ 1) for i in range(n_head)])

    payload = pl.pallas_call(
        payload_kernel,
        out_shape=shape((n_ctx, BLOCK, TOK), BF16),
        in_specs=[ANY, ANY],
        out_specs=ANY,
        scratch_shapes=[
            pltpu.VMEM((BLOCK, TOK), BF16),
            pltpu.VMEM((FULL, TOK), BF16),
            pltpu.VMEM((TOK, FULL), BF16),
            pltpu.VMEM((1, TOK), jnp.int32),
            pltpu.SemaphoreType.DMA((2,)),
            pltpu.SemaphoreType.DMA((n_ctx,)),
        ],
        compiler_params=vmem(2),
    )(lat_t, positions)
    recv_mine = lax.all_to_all(payload, "ctx", 0, 0)

    part_rows = heads * width
    start, lat_grad, lat_scaled, delta, key_mine, key_other, query_own, parts = pl.pallas_call(
        prologue_kernel,
        out_shape=[
            near_shape((8, TOK), F32),
            far_shape((heads, LATENT, TOK), BF16),
            far_shape((heads, LATENT, TOK), BF16),
            far_shape((heads, TOK), F32),
            far_shape((FULL, TOK), F32),
            far_shape((FULL, TOK), F32),
            far_shape((pairs, FULL, 2 * TOK), F32),
            far_shape((n_ctx, n_dp, part_rows, VHEAD), BF16),
        ],
        in_specs=[ANY] * 7,
        out_specs=[VM] + [ANY] * 7,
        scratch_shapes=[
            pltpu.VMEM((heads, FULL, TOK), BF16),
            pltpu.VMEM((heads, TOK), F32),
            pltpu.VMEM((heads, LATENT, TOK), BF16),
            pltpu.VMEM((heads, LATENT, TOK), BF16),
            pltpu.VMEM((heads, TOK), F32),
            pltpu.VMEM((TOK * heads, VHEAD), BF16),
            pltpu.VMEM((TOK * heads, LATENT), BF16),
            pltpu.VMEM((heads, LATENT, VHEAD), BF16),
            pltpu.VMEM((FULL, TOK), BF16),
            pltpu.VMEM((1, TOK), jnp.int32),
            pltpu.VMEM((TOK * heads, VHEAD), F32),
            pltpu.VMEM((2, TOK * heads, VHEAD), F32),
            pltpu.VMEM((n_ctx, n_dp, part_rows, VHEAD), F32),
            pltpu.VMEM((n_ctx, n_dp, part_rows, VHEAD), BF16),
            pltpu.VMEM((TOK, FULL), BF16),
            pltpu.VMEM((FULL, TOK), F32),
            pltpu.VMEM((FULL, TOK), F32),
            pltpu.VMEM((FULL, TOK), F32),
            pltpu.VMEM((pairs, FULL, 2 * TOK), F32),
            pltpu.SemaphoreType.DMA((7,)),
            pltpu.SemaphoreType.DMA((7,)),
        ],
        compiler_params=vmem(28),
        cost_estimate=cost(2 * heads * TOK * TOK * 1900, 8 << 20, heads * TOK * TOK),
    )(
        far_away(out_grad[0].reshape(TOK * heads, VHEAD)),
        far_away(saved_out[0].reshape(TOK * heads, LATENT)),
        far_away(value_up),
        q_t,
        lat_t,
        positions,
        lse_t,
    )
    recv_other = core_swap(recv_mine)

    held_shapes = [
        ((heads, FULL, TOK), BF16),
        ((heads, TOK), F32),
        ((heads, LATENT, TOK), BF16),
        ((heads, LATENT, TOK), BF16),
        ((heads, TOK), F32),
    ]

    def attend(recv, first, count, other, stage, last, operands, so_far, after):
        rows = count * HALF
        return pl.pallas_call(
            functools.partial(attention_kernel, first, last, stage),
            out_shape=[
                shape((heads, FULL, TOK), BF16) if last else near_shape((pairs, FULL, 2 * TOK), F32),
                shape((FULL, rows), BF16) if other else near_shape((FULL, rows), F32),
                near_shape((8, TOK), F32),
            ]
            + [near_shape(*h) for h in held_shapes if stage],
            in_specs=[ANY] * 2 + [ANY if stage else VM] * 5 + [ANY, ANY if stage else VM, VM],
            out_specs=[ANY if last else VM, VM, VM] + [VM] * (5 if stage else 0),
            scratch_shapes=[
                pltpu.VMEM((count, BLOCK, TOK), BF16),
                pltpu.VMEM((1, TOK), jnp.int32),
                pltpu.VMEM((FULL, TOK), F32),
                pltpu.VMEM((FULL, rows), F32),
                pltpu.VMEM((rows, FULL), BF16),
                pltpu.VMEM((FULL, rows), BF16),
                pltpu.VMEM((heads, FULL, TOK), BF16),
                pltpu.SemaphoreType.DMA((pairs,)),
                pltpu.SemaphoreType.DMA((24,)),
            ],
            input_output_aliases={} if stage or last else {8: 0},
            compiler_params=vmem(20),
            cost_estimate=cost(1 << 33, 1 << 16),
        )(
            recv, positions, *[far_away(x) if stage else held(x) for x in operands],
            far_away(key_other if other else key_mine), far_away(so_far) if stage else held(so_far), held(after),
        )

    near = n_ctx // 2
    query, sum_1, step, *staged = attend(
        recv_mine, 0, near, False, True, False, (q_t, lse_t, lat_grad, lat_scaled, delta), query_own, start
    )
    query, sum_2, step = attend(recv_other, 0, n_ctx, True, False, False, staged, query, step)
    sum_recv = core_swap(sum_2)
    query_grad, sum_3, step = attend(recv_mine, near, n_ctx - near, False, False, True, staged, query, step)

    weight_ctx = lax.all_to_all(parts, "ctx", 0, 0)
    packed = pl.pallas_call(
        pack_kernel,
        out_shape=shape((n_ctx, SPLIT, TOK), BF16),
        in_specs=[VM] * 3 + [ANY],
        out_specs=VM,
        compiler_params=vmem(6),
    )(held(sum_1), held(sum_3), sum_recv, weight_ctx)
    summed = lax.all_to_all(packed, "ctx", 0, 0)

    send_1, keep_1 = pl.pallas_call(
        weight_kernel,
        out_shape=[
            shape((2, part_rows, VHEAD), BF16),
            shape((2, part_rows, VHEAD), BF16),
        ],
        in_specs=[VM, ANY],
        out_specs=[VM] * 2,
        compiler_params=vmem(4),
        cost_estimate=cost(1 << 16, 1 << 16),
    )(weight_ctx, packed)

    recv_1 = lax.ppermute(send_1, "dp", [(i, i ^ 1) for i in range(n_dp)])
    stay, send_2 = pl.pallas_call(
        middle_kernel,
        out_shape=[shape((part_rows, VHEAD), F32), shape((part_rows, VHEAD), BF16)],
        in_specs=[VM] * 2,
        out_specs=[VM] * 2,
        compiler_params=vmem(2),
        cost_estimate=cost(1 << 16, 1 << 16),
    )(keep_1, recv_1)
    recv_2 = lax.ppermute(send_2, "dp", [(i, n_dp - 1 - i) for i in range(n_dp)])
    key_part = pl.pallas_call(
        sum_kernel,
        out_shape=shape((SPLIT, TOK), BF16),
        in_specs=[VM],
        out_specs=VM,
        compiler_params=vmem(4),
    )(summed)
    key_grad, weight_share = pl.pallas_call(
        last_kernel,
        out_shape=[shape((FULL, TOK), F32), shape((width, heads, VHEAD), F32)],
        in_specs=[VM] * 3,
        out_specs=[VM] * 2,
        scratch_shapes=[pltpu.VMEM((heads * width, VHEAD), F32)],
        compiler_params=vmem(2),
    )(lax.all_gather(key_part, "head"), stay, recv_2)
    return (jnp.transpose(query_grad, (2, 0, 1))[None], key_grad.T[None], weight_share)


def solution(mesh):
    return jax.shard_map(
        body,
        mesh=mesh,
        in_specs=(
            P("dp", "ctx", "head", None),
            P("dp", "ctx", None),
            P("dp", "ctx"),
            P("dp", "ctx", "head"),
            P("dp", "ctx", "head", None),
            P("dp", "ctx", "head", None),
            P("head", None, None),
        ),
        out_specs=(
            P("dp", "ctx", "head", None),
            P("dp", "ctx", None),
            P(("dp", "ctx"), "head", None),
        ),
        check_vma=False,
    )
```

```python
import functools

import jax
import jax.numpy as jnp
from jax import lax
from jax.experimental import pallas as pl
from jax.experimental.pallas import tpu as pltpu
from jax.sharding import PartitionSpec as P

ROPE = 32
VHEAD = 128
LATENT = 256
FULL = LATENT + ROPE
TOK = 128
HALF = TOK // 2
SCALING = (VHEAD + ROPE) ** -0.5
LOG2E = 1.4426950408889634
FAR = 1e30
ROT = 2 * HALF
RANK = ROT + HALF * ROPE // TOK
BLOCK = RANK + 16
SPLIT = FULL // 2
F32 = jnp.float32
BF16 = jnp.bfloat16
NT = (((1,), (1,)), ((), ()))
VM = pl.BlockSpec(memory_space=pltpu.VMEM)
ANY = pl.BlockSpec(memory_space=pl.ANY)
SM = pl.BlockSpec(memory_space=pltpu.SMEM)


def vmem(mib):
    return pltpu.CompilerParams(vmem_limit_bytes=mib << 20)


def cost(flops, nbytes, exps=0):
    return pl.CostEstimate(flops=flops, bytes_accessed=nbytes, transcendentals=exps)


def shape(dims, dtype):
    return jax.ShapeDtypeStruct(dims, dtype)


def near_shape(dims, dtype):
    return pltpu.VMEM(dims, dtype)


def far_shape(dims, dtype):
    return pltpu.HBM(dims, dtype)


def held(x):
    return pltpu.with_memory_space_constraint(x, pltpu.VMEM)


def far_away(x):
    return pltpu.with_memory_space_constraint(x, pltpu.HBM)


def dot(a, b):
    return jnp.dot(a, b, preferred_element_type=F32)


def dot_nt(a, b):
    return lax.dot_general(a, b, NT, preferred_element_type=F32)


def both(ref, pair):
    return jnp.concatenate([ref[2 * pair], ref[2 * pair + 1]], axis=1)


def both_rows(ref, pair):
    return jnp.concatenate([ref[pl.ds(2 * pair, 1), :], ref[pl.ds(2 * pair + 1, 1), :]], axis=1)


def payload_kernel(lat_hbm, pos_hbm, out_hbm, block, lat_s, key_s, pos_s, in_sem, out_sem):
    lat_in = pltpu.make_async_copy(lat_hbm, lat_s, in_sem.at[0])
    pos_in = pltpu.make_async_copy(pos_hbm, pos_s, in_sem.at[1])
    lat_in.start()
    pos_in.start()
    pos_in.wait()
    base = jnp.min(pos_s[...].astype(F32), axis=1, keepdims=True)
    block[RANK:] = jnp.broadcast_to(base * (1.0 / TOK), (BLOCK - RANK, TOK)).astype(BF16)
    lat_in.wait()
    key_s[...] = lat_s[...].T
    half = key_s[pl.ds(pl.multiple_of(lax.rem(lax.axis_index("head"), 2) * HALF, HALF), HALF), :]
    block[:HALF] = half[:, :TOK]
    block[HALF:ROT] = half[:, TOK:LATENT]
    rot = half[:, LATENT:].astype(F32)
    block[ROT:RANK] = jnp.concatenate([rot[16 * g : 16 * g + 16] for g in range(HALF // 16)], axis=1).astype(BF16)
    copies = [pltpu.make_async_copy(block, out_hbm.at[j], out_sem.at[j]) for j in range(out_hbm.shape[0])]
    for copy in copies:
        copy.start()
    for copy in copies:
        copy.wait()


def prologue_kernel(out_grad_hbm, saved_hbm, up_hbm, q_hbm, lat_hbm, pos_hbm, lse_hbm, *rest):
    start, lat_hbm_out, scaled_hbm, delta_hbm, mine_hbm, other_hbm, query_hbm, parts_hbm = rest[:8]
    queries, lse, lat_grad, lat_scaled, delta = rest[8:13]
    out_grad, saved, value_up, lat_ref, pos_ref, grad_s, saved_s, part_s, parts, key_s = rest[-16:-6]
    key_own, key_mine, key_other, query_own, sem, out_sem = rest[-6:]
    side = lax.rem(lax.axis_index("ctx"), 2)
    core = lax.rem(lax.axis_index("head"), 2)
    moves = [
        (out_grad_hbm, out_grad),
        (saved_hbm, saved),
        (up_hbm, value_up),
        (q_hbm, queries),
        (lat_hbm, lat_ref),
        (pos_hbm, pos_ref),
        (lse_hbm, lse),
    ]
    copies = [pltpu.make_async_copy(src, dst, sem.at[i]) for i, (src, dst) in enumerate(moves)]
    for copy in copies:
        copy.start()
    heads = queries.shape[0]
    n_ctx, n_dp = part_s.shape[:2]
    width = LATENT // (n_ctx * n_dp)
    copies[0].wait()
    grad_s[...] = out_grad[...].astype(F32)
    copies[1].wait()
    saved_s[0] = saved[:, :VHEAD].astype(F32)
    saved_s[1] = saved[:, VHEAD:].astype(F32)
    for copy in copies[2:]:
        copy.wait()

    def one(h, _):
        grad_h = grad_s[pl.ds(h, TOK, stride=heads), :].astype(BF16)
        saved_h = jnp.concatenate([saved_s[c, pl.ds(h, TOK, stride=heads), :].T for c in range(2)], axis=0)
        lat = dot_nt(value_up[h], grad_h)
        scaled = (lat * SCALING).astype(BF16)
        lat_grad[h] = lat.astype(BF16)
        lat_scaled[h] = scaled
        delta[pl.ds(h, 1), :] = jnp.sum(scaled.astype(F32) * saved_h, axis=0, keepdims=True)
        part = dot(saved_h.astype(BF16), grad_h)
        for d in range(n_dp):
            rows = part[d * n_ctx * width : (d + 1) * n_ctx * width]
            part_s[:, d, pl.ds(width * h, width), :] = rows.reshape(n_ctx, width, VHEAD)
        return 0

    lax.fori_loop(0, heads, one, 0, unroll=4)
    start[...] = jnp.zeros_like(start)
    outs = [
        (parts, parts_hbm),
        (lat_grad, lat_hbm_out),
        (lat_scaled, scaled_hbm),
        (delta, delta_hbm),
        (key_mine, mine_hbm),
        (key_other, other_hbm),
        (query_own, query_hbm),
    ]
    outs = [pltpu.make_async_copy(src, dst, out_sem.at[i]) for i, (src, dst) in enumerate(outs)]
    parts[...] = part_s[...].astype(BF16)
    for copy in outs[:4]:
        copy.start()

    key_s[...] = lat_ref[...].T
    pos_q = pos_ref[...].astype(F32)
    pos_k = jnp.broadcast_to(pos_q, (TOK, TOK)).T
    visible = pos_k <= jnp.broadcast_to(pos_q, (TOK, TOK))
    visible = jnp.concatenate([visible, visible], axis=1)
    key_own[...] = jnp.zeros_like(key_own)
    for pair in range(heads // 2):
        q2 = both(queries, pair)
        logits = dot(key_s[...], q2)
        weights = jnp.where(visible, jnp.exp2(logits * (SCALING * LOG2E) - both_rows(lse, pair) * LOG2E), 0.0)
        dot_value = dot(key_s[:, :LATENT], both(lat_scaled, pair))
        dl = (weights * (dot_value - both_rows(delta, pair))).astype(BF16)
        query_own[pair] = dot(lat_ref[...], dl)
        key_own[...] += dot_nt(q2, dl)
        key_own[:LATENT] += dot_nt(both(lat_grad, pair), weights.astype(BF16))
    here = lax.broadcasted_iota(jnp.int32, (FULL, TOK), 1) // HALF == side
    own = key_own[...]
    kept = jnp.where(here, own, 0.0)
    moved = jnp.where(here, jnp.concatenate([own[:, HALF:], own[:, :HALF]], axis=1), 0.0)
    key_mine[...] = jnp.where(core == side, kept, moved)
    key_other[...] = jnp.where(core == side, moved, kept)
    for copy in outs[4:]:
        copy.start()
    for copy in outs:
        copy.wait()


def attention_kernel(first, last, stage, *rest):
    recv_hbm, pos_hbm, *operands, own_hbm, so_far, after = rest[:10]
    query_out, key_out, done = rest[10:13]
    recv, pos, key_own, key_acc, key_s, keys_t, last_s, sem, in_sem = rest[-9:]
    queries, lse, lat_grad, lat_scaled, delta = rest[13:18] if stage else operands
    heads = queries.shape[0]
    count = key_s.shape[0] // HALF
    quarter = max(1, count // 4)
    copies = []

    def fetch(src, dst):
        copies.append(pltpu.make_async_copy(src, dst, in_sem.at[len(copies)]))
        copies[-1].start()
        return copies[-1]

    key_copies = [
        fetch(recv_hbm.at[first + lo : first + lo + quarter], recv.at[lo : lo + quarter])
        for lo in range(0, count, quarter)
    ]
    pos_copy = fetch(pos_hbm, pos)
    near = heads // 4
    groups = [[fetch(operands[1], lse), fetch(operands[4], delta)] if stage else []] + [[], [], []]
    for i in range(4):
        part = slice(near * i, near * i + near)
        if stage:
            groups[i] += [
                fetch(src.at[part], dst.at[part])
                for src, dst in ((operands[0], queries), (operands[3], lat_scaled), (operands[2], lat_grad))
            ]
            half = slice(near // 2 * i, near // 2 * (i + 1))
            groups[i].append(fetch(so_far.at[half], query_out.at[half]))
    own_copy = fetch(own_hbm, key_own)
    own = lax.axis_index("ctx")
    key_acc[...] = jnp.zeros_like(key_acc)
    for j in range(count):
        if j % quarter == 0:
            key_copies[j // quarter].wait()
        lo = HALF * j
        key_s[lo : lo + HALF, :TOK] = recv[j, :HALF]
        key_s[lo : lo + HALF, TOK:LATENT] = recv[j, HALF:ROT]
        rot = recv[j, ROT:RANK].astype(F32)
        for g in range(HALF // 16):
            key_s[lo + 16 * g : lo + 16 * g + 16, LATENT:] = rot[:, ROPE * g : ROPE * g + ROPE].astype(BF16)
    pos_copy.wait()
    rank_q = jnp.min(pos[...].astype(F32), axis=1, keepdims=True) * (1.0 / TOK)
    far = []
    for j in range(count):
        one_far = jnp.where(recv[j, RANK : RANK + 1, :].astype(F32) < rank_q, 0.0, FAR)
        far.append(jnp.concatenate([one_far, one_far], axis=1))
    def copy_out(pair):
        part = pl.ds(2 * pair, 2)
        return pltpu.make_async_copy(last_s.at[part], query_out.at[part], sem.at[pair])

    def one(pair, _):
        q2 = both(queries, pair)
        logits = dot(key_s[...], q2)
        dot_value = dot(key_s[:, :LATENT], both(lat_scaled, pair))
        lse2 = both_rows(lse, pair) * LOG2E
        delta2 = both_rows(delta, pair)
        weights = jnp.concatenate(
            [
                jnp.exp2(logits[HALF * j : HALF * j + HALF] * (SCALING * LOG2E) - (lse2 + far[j]))
                for j in range(count)
            ],
            axis=0,
        )
        dl = (weights * (dot_value - delta2)).astype(BF16)
        grad = (query_out if stage else so_far)[pair] + dot(keys_t[...], dl)
        if last:
            last_s[2 * pair] = grad[:, :TOK].astype(BF16)
            last_s[2 * pair + 1] = grad[:, TOK:].astype(BF16)
            copy_out(pair).start()
        else:
            query_out[pair] = grad
        key_acc[:LATENT] += dot_nt(
            jnp.concatenate([q2[:LATENT], both(lat_grad, pair)], axis=1),
            jnp.concatenate([dl, weights.astype(BF16)], axis=1),
        )
        key_acc[LATENT:] += dot_nt(q2[LATENT:], dl)
        return 0

    for lo in range(0, count * HALF, TOK):
        keys_t[:, lo : lo + TOK] = key_s[lo : lo + TOK, :].T
    steps = 2 if stage else 1
    for i in range(steps):
        for copy in groups[2 * i] + groups[2 * i + 1]:
            copy.wait()
        each = heads // 2 // steps
        lax.fori_loop(each * i, each * i + each, one, 0, unroll=each)
    own_copy.wait()
    for t in range(count * HALF // TOK):
        total = key_acc[:, TOK * t : TOK * t + TOK]
        total = total + jnp.where(own // 2 == first // 2 + t, 1.0, 0.0) * key_own[...]
        key_out[:, TOK * t : TOK * t + TOK] = total.astype(key_out.dtype)
    done[...] = after[: done.shape[0]]
    if last:
        for pair in range(heads // 2):
            copy_out(pair).wait()


def pack_kernel(mine_1, mine_2, recv, after, out_ref):
    del after
    t = 0
    for ref in (mine_1, mine_2):
        for i in range(ref.shape[1] // TOK):
            tile = ref[:, TOK * i : TOK * i + TOK] + recv[:, TOK * t : TOK * t + TOK].astype(F32)
            low, high = tile[:SPLIT], tile[SPLIT:]
            out_ref[2 * t] = jnp.concatenate([low[:, :HALF], high[:, :HALF]], axis=1).astype(BF16)
            out_ref[2 * t + 1] = jnp.concatenate([low[:, HALF:], high[:, HALF:]], axis=1).astype(BF16)
            t += 1


def weight_kernel(recv, after, friend_ref, keep_ref):
    del after
    total = recv[0].astype(F32)
    for j in range(1, recv.shape[0]):
        total = total + recv[j].astype(F32)
    dp = lax.axis_index("dp")
    friend = dp + 1 - 2 * lax.rem(dp, 2)
    for ref, index in ((friend_ref, friend), (keep_ref, dp)):
        for i, part in enumerate((index, recv.shape[1] - 1 - index)):
            chosen = total[0]
            for d in range(1, recv.shape[1]):
                chosen = jnp.where(part == d, total[d], chosen)
            ref[i] = chosen.astype(BF16)


def middle_kernel(keep, recv, stay_ref, send_ref):
    total = keep[...].astype(F32) + recv[...].astype(F32)
    stay_ref[...] = total[0]
    send_ref[...] = total[1].astype(BF16)


def sum_kernel(recv, key_ref):
    total = recv[0].astype(F32)
    for j in range(1, recv.shape[0]):
        total = total + recv[j].astype(F32)
    key_ref[...] = total.astype(BF16)


def last_kernel(parts, stay, weight_recv, out_ref, weight_ref, part_s):
    part_s[...] = stay[...] + weight_recv[...].astype(F32)
    width, heads = weight_ref.shape[0], weight_ref.shape[1]
    for i in range(width):
        weight_ref[i] = part_s[pl.ds(i, heads, stride=width), :]
    sides = []
    for core in range(2):
        total = parts[core].astype(F32)
        for other in range(core + 2, parts.shape[0], 2):
            total = total + parts[other].astype(F32)
        sides.append(total)
    out_ref[:SPLIT] = jnp.concatenate([sides[0][:, :HALF], sides[1][:, :HALF]], axis=1)
    out_ref[SPLIT:] = jnp.concatenate([sides[0][:, HALF:], sides[1][:, HALF:]], axis=1)


def body(queries, latents, positions, lse, saved_out, out_grad, value_up):
    n_dp, n_ctx, n_head = lax.axis_size("dp"), lax.axis_size("ctx"), lax.axis_size("head")
    heads = queries.shape[2]
    groups = n_dp * n_ctx
    width = LATENT // groups
    pairs = heads // 2
    q_t = far_away(jnp.transpose(queries[0], (1, 2, 0)))
    lat_t = far_away(latents[0].T)
    lse_t = far_away(lse[0].T)
    positions = far_away(positions)
    def core_swap(x):
        return lax.ppermute(x, "head", [(i, i ^ 1) for i in range(n_head)])

    payload = pl.pallas_call(
        payload_kernel,
        out_shape=shape((n_ctx, BLOCK, TOK), BF16),
        in_specs=[ANY, ANY],
        out_specs=ANY,
        scratch_shapes=[
            pltpu.VMEM((BLOCK, TOK), BF16),
            pltpu.VMEM((FULL, TOK), BF16),
            pltpu.VMEM((TOK, FULL), BF16),
            pltpu.VMEM((1, TOK), jnp.int32),
            pltpu.SemaphoreType.DMA((2,)),
            pltpu.SemaphoreType.DMA((n_ctx,)),
        ],
        compiler_params=vmem(2),
    )(lat_t, positions)
    recv_mine = lax.all_to_all(payload, "ctx", 0, 0)

    part_rows = heads * width
    start, lat_grad, lat_scaled, delta, key_mine, key_other, query_own, parts = pl.pallas_call(
        prologue_kernel,
        out_shape=[
            near_shape((8, TOK), F32),
            far_shape((heads, LATENT, TOK), BF16),
            far_shape((heads, LATENT, TOK), BF16),
            far_shape((heads, TOK), F32),
            far_shape((FULL, TOK), F32),
            far_shape((FULL, TOK), F32),
            far_shape((pairs, FULL, 2 * TOK), F32),
            far_shape((n_ctx, n_dp, part_rows, VHEAD), BF16),
        ],
        in_specs=[ANY] * 7,
        out_specs=[VM] + [ANY] * 7,
        scratch_shapes=[
            pltpu.VMEM((heads, FULL, TOK), BF16),
            pltpu.VMEM((heads, TOK), F32),
            pltpu.VMEM((heads, LATENT, TOK), BF16),
            pltpu.VMEM((heads, LATENT, TOK), BF16),
            pltpu.VMEM((heads, TOK), F32),
            pltpu.VMEM((TOK * heads, VHEAD), BF16),
            pltpu.VMEM((TOK * heads, LATENT), BF16),
            pltpu.VMEM((heads, LATENT, VHEAD), BF16),
            pltpu.VMEM((FULL, TOK), BF16),
            pltpu.VMEM((1, TOK), jnp.int32),
            pltpu.VMEM((TOK * heads, VHEAD), F32),
            pltpu.VMEM((2, TOK * heads, VHEAD), F32),
            pltpu.VMEM((n_ctx, n_dp, part_rows, VHEAD), F32),
            pltpu.VMEM((n_ctx, n_dp, part_rows, VHEAD), BF16),
            pltpu.VMEM((TOK, FULL), BF16),
            pltpu.VMEM((FULL, TOK), F32),
            pltpu.VMEM((FULL, TOK), F32),
            pltpu.VMEM((FULL, TOK), F32),
            pltpu.VMEM((pairs, FULL, 2 * TOK), F32),
            pltpu.SemaphoreType.DMA((7,)),
            pltpu.SemaphoreType.DMA((7,)),
        ],
        compiler_params=vmem(28),
        cost_estimate=cost(2 * heads * TOK * TOK * 1900, 8 << 20, heads * TOK * TOK),
    )(
        far_away(out_grad[0].reshape(TOK * heads, VHEAD)),
        far_away(saved_out[0].reshape(TOK * heads, LATENT)),
        far_away(value_up),
        q_t,
        lat_t,
        positions,
        lse_t,
    )
    recv_other = core_swap(recv_mine)

    held_shapes = [
        ((heads, FULL, TOK), BF16),
        ((heads, TOK), F32),
        ((heads, LATENT, TOK), BF16),
        ((heads, LATENT, TOK), BF16),
        ((heads, TOK), F32),
    ]

    def attend(recv, first, count, other, stage, last, operands, so_far, after):
        rows = count * HALF
        return pl.pallas_call(
            functools.partial(attention_kernel, first, last, stage),
            out_shape=[
                shape((heads, FULL, TOK), BF16) if last else near_shape((pairs, FULL, 2 * TOK), F32),
                shape((FULL, rows), BF16) if other else near_shape((FULL, rows), F32),
                near_shape((8, TOK), F32),
            ]
            + [near_shape(*h) for h in held_shapes if stage],
            in_specs=[ANY] * 2 + [ANY if stage else VM] * 5 + [ANY, ANY if stage else VM, VM],
            out_specs=[ANY if last else VM, VM, VM] + [VM] * (5 if stage else 0),
            scratch_shapes=[
                pltpu.VMEM((count, BLOCK, TOK), BF16),
                pltpu.VMEM((1, TOK), jnp.int32),
                pltpu.VMEM((FULL, TOK), F32),
                pltpu.VMEM((FULL, rows), F32),
                pltpu.VMEM((rows, FULL), BF16),
                pltpu.VMEM((FULL, rows), BF16),
                pltpu.VMEM((heads, FULL, TOK), BF16),
                pltpu.SemaphoreType.DMA((pairs,)),
                pltpu.SemaphoreType.DMA((24,)),
            ],
            input_output_aliases={} if stage or last else {8: 0},
            compiler_params=vmem(20),
            cost_estimate=cost(1 << 33, 1 << 16),
        )(
            recv, positions, *[far_away(x) if stage else held(x) for x in operands],
            far_away(key_other if other else key_mine), far_away(so_far) if stage else held(so_far), held(after),
        )

    near = n_ctx // 2
    query, sum_1, step, *staged = attend(
        recv_mine, 0, near, False, True, False, (q_t, lse_t, lat_grad, lat_scaled, delta), query_own, start
    )
    query, sum_2, step = attend(recv_other, 0, n_ctx, True, False, False, staged, query, step)
    sum_recv = core_swap(sum_2)
    query_grad, sum_3, step = attend(recv_mine, near, n_ctx - near, False, False, True, staged, query, step)

    weight_ctx = lax.all_to_all(parts, "ctx", 0, 0)
    packed = pl.pallas_call(
        pack_kernel,
        out_shape=shape((n_ctx, SPLIT, TOK), BF16),
        in_specs=[VM] * 3 + [ANY],
        out_specs=VM,
        compiler_params=vmem(6),
    )(held(sum_1), held(sum_3), sum_recv, weight_ctx)
    summed = lax.all_to_all(packed, "ctx", 0, 0)

    send_1, keep_1 = pl.pallas_call(
        weight_kernel,
        out_shape=[
            shape((2, part_rows, VHEAD), BF16),
            shape((2, part_rows, VHEAD), BF16),
        ],
        in_specs=[VM, ANY],
        out_specs=[VM] * 2,
        compiler_params=vmem(4),
        cost_estimate=cost(1 << 16, 1 << 16),
    )(weight_ctx, packed)

    recv_1 = lax.ppermute(send_1, "dp", [(i, i ^ 1) for i in range(n_dp)])
    stay, send_2 = pl.pallas_call(
        middle_kernel,
        out_shape=[shape((part_rows, VHEAD), F32), shape((part_rows, VHEAD), BF16)],
        in_specs=[VM] * 2,
        out_specs=[VM] * 2,
        compiler_params=vmem(2),
        cost_estimate=cost(1 << 16, 1 << 16),
    )(keep_1, recv_1)
    recv_2 = lax.ppermute(send_2, "dp", [(i, n_dp - 1 - i) for i in range(n_dp)])
    key_part = pl.pallas_call(
        sum_kernel,
        out_shape=shape((SPLIT, TOK), BF16),
        in_specs=[VM],
        out_specs=VM,
        compiler_params=vmem(4),
    )(summed)
    key_grad, weight_share = pl.pallas_call(
        last_kernel,
        out_shape=[shape((FULL, TOK), F32), shape((width, heads, VHEAD), F32)],
        in_specs=[VM] * 3,
        out_specs=[VM] * 2,
        scratch_shapes=[pltpu.VMEM((heads * width, VHEAD), F32)],
        compiler_params=vmem(2),
    )(lax.all_gather(key_part, "head"), stay, recv_2)
    return (jnp.transpose(query_grad, (2, 0, 1))[None], key_grad.T[None], weight_share)


def solution(mesh):
    return jax.shard_map(
        body,
        mesh=mesh,
        in_specs=(
            P("dp", "ctx", "head", None),
            P("dp", "ctx", None),
            P("dp", "ctx"),
            P("dp", "ctx", "head"),
            P("dp", "ctx", "head", None),
            P("dp", "ctx", "head", None),
            P("head", None, None),
        ),
        out_specs=(
            P("dp", "ctx", "head", None),
            P("dp", "ctx", None),
            P(("dp", "ctx"), "head", None),
        ),
        check_vma=False,
    )
```
